256 devices in a mesh: dp: 32 (over x, y, core), mp: 8 (over z).
Axes of the slice: x: 4, y: 4, z: 8, core: 2. Of those that a mesh axis runs over, the one named last changes fastest.
Arguments:
- hidden_first: bfloat16 [6144, 4096], P('dp'), may hold values from -256 to 256, as said below
- hidden_second: bfloat16 [6144, 4096], P('dp'), may hold values from -256 to 256, as said below
- weight: bfloat16 [4096, 4096], P('dp', 'mp'), may hold values from -0.09375 to 0.09375
Outputs:
- grad_weight: bfloat16 [4096, 4096], P('dp', 'mp')
- grad_first: bfloat16 [6144, 4096], P('dp', 'mp')
- grad_second: bfloat16 [6144, 4096], P('dp', 'mp')
The draws below stay inside these ranges and needn't reach their ends.
Inputs may be any that keep to these rules, and one draw needn't show every extreme that they name: `hidden_first`: hidden activations of two augmented views of the same molecules. `hidden_second`: hidden activations of two augmented views of the same molecules.
All inputs are finite; a program needn't handle non-finite values.
Results may differ from the reference program's by a relative error of at most 0.023.
Values may be sent and summed in bfloat16 or wider, within the bound.
A program may use at most 64 MiB of HBM per device.

```python
import math
import jax
import jax.numpy as jnp
from jax import lax

H = 4096
D = 4096
TOK_DEV = 192
TOKENS = 6144
N_DP = 32
N_MP = 8


def clipped_normal(key, shape):
    return jnp.clip(jax.random.normal(key, shape, jnp.float32), -4.0, 4.0)


def shared_parts(key):
    keys = jax.random.split(key, 7)
    position = jnp.arange(TOKENS, dtype=jnp.float32) / max(TOKENS - 1, 1)
    trend = (0.5 + position)[:, None]
    spread = jnp.exp(jax.random.uniform(keys[0], (TOKENS, 1), jnp.float32, math.log(0.3), math.log(3.0)))
    factor = clipped_normal(keys[1], (TOKENS, 1))
    loading = clipped_normal(keys[2], (1, H))
    offset = 0.7 * clipped_normal(keys[3], (1, H))
    content = clipped_normal(keys[4], (TOKENS, H))
    column_scale = jnp.exp(jax.random.uniform(keys[5], (1, H), jnp.float32, math.log(0.0625), math.log(4.0)))
    noise_level = jnp.exp(jax.random.uniform(keys[6], (1, H), jnp.float32, math.log(0.1), math.log(0.4)))
    return (trend, spread, factor, loading, offset, content, column_scale, noise_level)


def build_view(key, own, factor_weight):
    trend, spread, factor, loading, offset, content, column_scale, noise_level = shared_parts(key)
    inner = content + noise_level * own + factor_weight * factor * loading
    return (trend * (spread * column_scale * inner + offset)).astype(jnp.bfloat16)


def draw_hidden_first(key, part):
    base = key
    key = jax.random.fold_in(key, 11)
    own = clipped_normal(key, (TOKENS, H))
    return build_view(base, own, 0.3)


def draw_hidden_second(key, part):
    base = key
    key = jax.random.fold_in(key, 23)
    own = clipped_normal(key, (TOKENS, H))
    return build_view(base, own, 0.3)


def block_levels(key, shape, pieces, smallest, high):
    def one(dim, blocks):
        draws = jax.random.uniform(jax.random.fold_in(jax.random.fold_in(key, 6), dim), (blocks,), jnp.float32, smallest / len(pieces), high / len(pieces))
        return jnp.repeat(jnp.exp(draws), shape[dim] // blocks).reshape((-1,) + (1,) * (len(shape) - dim - 1))

    gain = one(*pieces[0])
    for cut in pieces[1:]:
        gain = gain * one(*cut)
    return gain


def normal_values(key, dims, deviation, reach, cuts=(), kind=jnp.bfloat16):
    entries = jax.random.normal(key, dims, jnp.float32) * deviation
    if len(cuts) > 0:
        entries = block_levels(key, dims, cuts, -0.22, 0.18) * entries
    return jnp.clip(entries, min=-reach, max=reach).astype(kind)


def setup_inputs(seed: int = 0) -> dict:
    splits = jax.random.split(jax.random.key(seed), 4)
    return {
        "hidden_first": draw_hidden_first(jax.random.fold_in(splits[3], 71), 0),
        "hidden_second": draw_hidden_second(jax.random.fold_in(splits[3], 71), 0),
        "weight": normal_values(splits[2], (H, D), H ** -0.5, 0.09375, ((0, 32), (1, 8))),
    }


epsilon = 1e-05
offdiag_weight = 0.0051

def normalize(projected):
    center = lax.optimization_barrier(jnp.mean(projected, axis=0))
    shifted = projected - center
    variance = lax.optimization_barrier(jnp.mean(shifted * shifted, axis=0))
    spread = jnp.sqrt(variance + epsilon)
    return (((projected - center) / spread).astype(jnp.bfloat16), spread)

def backnorm(upstream, normed, spread):
    normed_f = normed.astype(jnp.float32)
    level = lax.optimization_barrier(jnp.mean(upstream, axis=0))
    slope = lax.optimization_barrier(jnp.mean(upstream * normed_f, axis=0))
    return ((upstream - level - normed_f * slope) / spread).astype(jnp.bfloat16)

def hidden_back(down, weight):
    columns = D // N_MP
    total = jnp.zeros((down.shape[0], weight.shape[0]), jnp.float32)
    for index in range(N_MP):
        part = jnp.dot(down[:, index * columns:(index + 1) * columns], weight[:, index * columns:(index + 1) * columns].T, preferred_element_type=jnp.float32)
        total = total + part.astype(jnp.bfloat16).astype(jnp.float32)
    return total.astype(jnp.bfloat16)

def reference(hidden_first, hidden_second, weight):
    project_first = jnp.dot(hidden_first, weight, preferred_element_type=jnp.float32)
    project_second = jnp.dot(hidden_second, weight, preferred_element_type=jnp.float32)
    norm_first, spread_first = normalize(project_first)
    norm_second, spread_second = normalize(project_second)
    crossed = jnp.dot(norm_first.T, norm_second, preferred_element_type=jnp.float32) / TOKENS
    diagonal_mask = jnp.eye(D, dtype=bool)
    loss_grad = jnp.where(diagonal_mask, 2.0 * (crossed - 1.0), 2.0 * offdiag_weight * crossed).astype(jnp.bfloat16)
    upstream_first = jnp.dot(norm_second, loss_grad.T, preferred_element_type=jnp.float32)
    upstream_second = jnp.dot(norm_first, loss_grad, preferred_element_type=jnp.float32)
    down_first = backnorm(upstream_first, norm_first, spread_first)
    down_second = backnorm(upstream_second, norm_second, spread_second)
    grad_first = hidden_back(down_first, weight)
    grad_second = hidden_back(down_second, weight)
    total = jnp.zeros((H, D), jnp.float32)
    for index in range(N_DP):
        low = index * TOK_DEV
        high = low + TOK_DEV
        term = jnp.dot(hidden_first[low:high].T, down_first[low:high], preferred_element_type=jnp.float32)
        term = term + jnp.dot(hidden_second[low:high].T, down_second[low:high], preferred_element_type=jnp.float32)
        total = total + term.astype(jnp.bfloat16).astype(jnp.float32)
    grad_weight = (total / math.sqrt(TOKENS)).astype(jnp.bfloat16)
    return (grad_weight, grad_first, grad_second)
```

```python
import math

import jax
import jax.numpy as jnp
from jax import lax
from jax.experimental import pallas as pl
from jax.experimental.pallas import tpu as pltpu
from jax.sharding import PartitionSpec as P

MESH = pl.DeviceIdType.MESH
BF = jnp.bfloat16
F32 = jnp.float32

epsilon = 1e-05
offdiag_weight = 0.0051

TOKENS = 6144
ROWS = 192
PAD = 208
COLS = 512
NZ = 8


def wrap(value, size):
    return lax.rem(value + size, size)


class Place:
    def __init__(self):
        dp = lax.axis_index("dp")
        self.dp = dp
        self.x = lax.div(dp, 8)
        self.y = lax.rem(lax.div(dp, 2), 4)
        self.c = lax.rem(dp, 2)
        self.z = lax.axis_index("mp")

    def X(self, d):
        return wrap(self.x + d, 4)

    def Y(self, d):
        return wrap(self.y + d, 4)

    def Z(self, d):
        return wrap(self.z + d, NZ)

    def block(self, dx, dy, dc=0):
        return self.X(dx) * 8 + self.Y(dy) * 2 + wrap(self.c + dc, 2)

    def at(self, dx, dy, dc=0):
        return {"dp": self.block(dx, dy, dc)}

    def sib(self):
        return {"dp": self.dp + 1 - 2 * self.c}

    def up(self, d):
        return {"mp": self.Z(d)}

    def plane_peers(self):
        row = [(0, dy, dc) for dy in range(4) for dc in range(2)][1:]
        column = [(dx, 0, 0) for dx in range(1, 4)]
        return [self.at(*p) for p in row + column]

    def z_peers(self):
        return [self.up(d) for d in range(1, NZ)]


class Net:
    def __init__(self, sends, recvs):
        self.sends, self.recvs = sends, recvs
        self.copies = []

    def send(self, src, dst, to):
        index = len(self.copies)
        copy = pltpu.make_async_remote_copy(
            src_ref=src,
            dst_ref=dst,
            send_sem=self.sends.at[index],
            recv_sem=self.recvs.at[index],
            device_id=to,
            device_id_type=MESH,
        )
        copy.start()
        self.copies.append(copy)
        return copy

    def drain(self):
        for copy in self.copies:
            copy.wait_send()


def barrier(peers):
    sem = pltpu.get_barrier_semaphore()
    for peer in peers:
        pl.semaphore_signal(sem, inc=1, device_id=peer, device_id_type=MESH)
    pl.semaphore_wait(sem, len(peers))


def dot(a, b, dims):
    return lax.dot_general(a, b, ((dims[0], dims[1]), ((), ())), preferred_element_type=F32)


def turn(o, first, second):
    return (first, second) if o == 0 else (second, first)


def gather_plane(net, me, W):
    def block(o, a, b):
        return me.block(*turn(o, a, b))

    def to(o, a, b):
        return me.at(*turn(o, a, b))

    def push(index, start, size, target):
        ref = W.at[index, pl.ds(start, size)]
        return net.send(ref, ref, target)

    own = me.block(0, 0)
    both = [(o, d) for d in (1, -1) for o in (0, 1)]
    first, second, half, far, sibs = {}, {}, {}, {}, []

    def over(o, a):
        for d in (1, -1):
            second[o, a, d] = push(block(o, a, 0), 64 * o, 64, to(o, 0, d))

    def share(o, a, b):
        sibs.append(push(block(o, a, b), 64 * o, 64, me.sib()))

    for o, d in both:
        first[o, d] = push(own, 64 * o, 64, to(o, d, 0))
    for o in (0, 1):
        over(o, 0)
    sibs.append(net.send(W.at[own], W.at[own], me.sib()))
    for o, d in both:
        first[o, d].wait_recv()
        half[o, d] = push(block(o, -d, 0), 64 * o + (0 if d == 1 else 32), 32, to(o, d, 0))
    for o, d in both:
        over(o, -d)
    for o, d in both:
        share(o, -d, 0)
    for o in (0, 1):
        half[o, 1].wait_recv()
        half[o, -1].wait_recv()
        over(o, 2)
        share(o, 2, 0)
    for a in (0, -1, 1, 2):
        for o, d in both:
            second[o, a, d].wait_recv()
            far[o, a, d] = push(
                block(o, a, -d), 64 * o + (0 if d == 1 else 32), 32, to(o, 0, d)
            )
            share(o, a, -d)
    for a in (0, -1, 1, 2):
        for o in (0, 1):
            far[o, a, 1].wait_recv()
            far[o, a, -1].wait_recv()
            share(o, a, 2)
    for copy in sibs:
        copy.wait_recv()


def scatter_plane(net, me, S, M1, F1, Q, M2, F2):
    def index(o, d):
        return me.X(d) if o == 0 else me.Y(d)

    def other(o, d):
        return me.Y(d) if o == 0 else me.X(d)

    def part(o, d, start, size=2):
        rows = pl.ds(64 * o, 64)
        if o == 0:
            return (index(o, d), pl.ds(start, size), rows)
        return (pl.ds(start, size), index(o, d), rows)

    def to(o, a, b):
        return me.at(*turn(o, a, b))

    both = [(o, d) for d in (1, -1) for o in (0, 1)]
    slot = {1: 0, -1: 1}
    mid, early, late = {}, {}, {}
    for o, d in both:
        h = 0 if d == 1 else 2
        mid[o, d] = net.send(S.at[part(o, 2, h)], M1.at[o, slot[d]], to(o, d, 0))
    for o, d in both:
        h = 0 if d == 1 else 2
        early[o, d] = net.send(
            S.at[part(o, d, 2 - h)], F1.at[o, slot[d], pl.ds(2 - h, 2)], to(o, d, 0)
        )
    for o, d in both:
        h = 0 if d == 1 else 2
        mid[o, d].wait_recv()
        S[part(o, d, h)] += M1[o, slot[d]]
        late[o, d] = net.send(S.at[part(o, d, h)], F1.at[o, slot[d], pl.ds(h, 2)], to(o, d, 0))
    mid2, early2, late2 = {}, {}, {}
    for o in (0, 1):
        for d in (1, -1):
            early[o, d].wait_recv()
            late[o, d].wait_recv()
        total = S[part(o, 0, 0, 4)].astype(F32) + F1[o, 0].astype(F32) + F1[o, 1].astype(F32)
        Q[o] = total.astype(BF)
        for d in (1, -1):
            h = 0 if d == 1 else 32
            mid2[o, d] = net.send(
                Q.at[o, other(o, 2), pl.ds(h, 32)], M2.at[o, slot[d]], to(o, 0, d)
            )
        for d in (1, -1):
            h = 0 if d == 1 else 32
            early2[o, d] = net.send(
                Q.at[o, other(o, d), pl.ds(32 - h, 32)],
                F2.at[o, slot[d], pl.ds(32 - h, 32)],
                to(o, 0, d),
            )
    for o in (0, 1):
        for d in (1, -1):
            h = 0 if d == 1 else 32
            mid2[o, d].wait_recv()
            Q[o, other(o, d), pl.ds(h, 32)] += M2[o, slot[d]]
            late2[o, d] = net.send(
                Q.at[o, other(o, d), pl.ds(h, 32)], F2.at[o, slot[d], pl.ds(h, 32)], to(o, 0, d)
            )
    result = []
    for o in (0, 1):
        for d in (1, -1):
            early2[o, d].wait_recv()
            late2[o, d].wait_recv()
        result.append(
            Q[o, other(o, 0)].astype(F32) + F2[o, 0].astype(F32) + F2[o, 1].astype(F32)
        )
    return result


def scatter_plane_scratch():
    return [
        pltpu.VMEM((2, 2, 2, 64, COLS), BF),
        pltpu.VMEM((2, 2, 4, 64, COLS), BF),
        pltpu.VMEM((2, 4, 64, COLS), BF),
        pltpu.VMEM((2, 2, 32, COLS), BF),
        pltpu.VMEM((2, 2, 64, COLS), BF),
    ]


class ScatterZ:
    def __init__(self, net, me, T, R, rows):
        self.net, self.me, self.T, self.R = net, me, T, R
        self.half = rows // 2
        self.copies = {}

    def slice(self, half):
        return pl.ds(half * self.half, self.half)

    def send(self, d, s, half):
        slot = 0 if d == 1 else 1
        index = self.me.Z(d * (4 - s))
        rows = self.slice(half)
        previous = self.copies.get((d, s - 1, half))
        if previous is not None:
            previous.wait_recv()
            self.T[index, rows] += self.R[slot, s - 1, rows]
        self.copies[d, s, half] = self.net.send(
            self.T.at[index, rows], self.R.at[slot, s, rows], self.me.up(d)
        )

    def long(self, s):
        self.send(1, s, 0)
        self.send(-1, s, 1)

    def short(self, s):
        self.send(1, s, 1)
        self.send(-1, s, 0)

    def finish(self, half):
        for d in (1, -1):
            self.copies[d, 3, half].wait_recv()
        rows = self.slice(half)
        return self.R[0, 3, rows].astype(F32) + self.R[1, 3, rows].astype(F32)


def exchange(net, me, B1, B2, merge1, merge2):
    copies = []
    for dy in range(4):
        for dc in range(2):
            if dy + dc > 0:
                copies.append(net.send(B1.at[0], B1.at[2 * dy + dc], me.at(0, dy, dc)))

    def middle():
        for copy in copies:
            copy.wait_recv()
        B2[0] = merge1(B1)
        return [net.send(B2.at[0], B2.at[dx], me.at(dx, 0, 0)) for dx in range(1, 4)]

    def last(second):
        for copy in second:
            copy.wait_recv()
        return merge2(B2)

    return middle, last


def merge_moments(rows):
    def merge(B):
        count = B.shape[0]
        result = []
        for view in range(2):
            means = [B[k, 2 * view : 2 * view + 1] for k in range(count)]
            squares = [B[k, 2 * view + 1 : 2 * view + 2] for k in range(count)]
            mean = sum(means) / count
            square = sum(squares) + rows * sum((m - mean) * (m - mean) for m in means)
            result += [mean, square]
        return jnp.concatenate(result, axis=0)

    return merge


def merge_sums(B):
    return sum(B[k] for k in range(B.shape[0]))


def project_kernel(hf, hs, w, W, normed, spread, acc, B1, B2, ssem, rsem):
    me = Place()
    barrier(me.plane_peers())
    net = Net(ssem, rsem)
    W[me.block(0, 0)] = w[...]
    gather_plane(net, me, W)
    acc[...] = jnp.zeros_like(acc)

    def body(k, _):
        cols = pl.ds(pl.multiple_of(k * 512, 512), 512)
        piece = W[pl.ds(4 * k, 4)].reshape(512, COLS)
        acc[0] += jnp.dot(hf[:, cols], piece, preferred_element_type=F32)
        acc[1] += jnp.dot(hs[:, cols], piece, preferred_element_type=F32)
        return 0

    lax.fori_loop(0, 8, body, 0)
    for view in range(2):
        mean = jnp.sum(acc[view], axis=0, keepdims=True) / ROWS
        shifted = acc[view] - mean
        B1[0, 2 * view : 2 * view + 1] = mean
        B1[0, 2 * view + 1 : 2 * view + 2] = jnp.sum(shifted * shifted, axis=0, keepdims=True)
    middle, last = exchange(net, me, B1, B2, merge_moments(ROWS), merge_moments(8 * ROWS))
    moments = last(middle())
    for view in range(2):
        mean = moments[2 * view : 2 * view + 1]
        deviation = jnp.sqrt(moments[2 * view + 1 : 2 * view + 2] / TOKENS + epsilon)
        spread[view : view + 1] = deviation
        normed[view] = ((acc[view] - mean) / deviation).astype(BF)
    net.drain()


def pair_send(net, me, Pb, S, b):
    where = (lax.div(b, 2), pl.ds(2 * lax.rem(b, 2), 2))
    return net.send(Pb.at[where + (1 - me.c,)], S.at[where], me.sib())


def pair_add(me, Pb, S, b):
    where = (lax.div(b, 2), pl.ds(2 * lax.rem(b, 2), 2))
    S[where] += Pb[where + (me.c,)]


def store_block(Pb, b, value):
    Pb[lax.div(b, 2), pl.ds(2 * lax.rem(b, 2), 2)] = value.astype(BF).reshape(2, 2, 128, COLS)


def corr_kernel(normed, A, N, G, D, Pb, S, M1, F1, Q, M2, F2, B1, B2, E, ssem, rsem):
    me = Place()
    barrier(me.plane_peers() + me.z_peers())
    net = Net(ssem, rsem)
    A[me.z, 0:ROWS] = normed[1]
    N[0:ROWS] = normed[0]
    passed = {}

    def pass_on(s):
        for half in (0, 1):
            for d in (1, -1):
                if s < 3 or half == (0 if d == 1 else 1):
                    ref = A.at[me.Z(-d * s), pl.ds(96 * half, 96)]
                    passed[s, d, half] = net.send(ref, ref, me.up(d))

    pairs = []

    def correlate(b):
        store_block(Pb, b, dot(A[b, 0:ROWS], N[0:ROWS], ((0,), (0,))))
        pairs.append((pair_send(net, me, Pb, S, b), b))

    pass_on(0)
    n1, n2 = normed[0].astype(F32), normed[1].astype(F32)
    B1[0, 0:1] = jnp.sum(n1, axis=0, keepdims=True)
    B1[0, 1:2] = jnp.sum(n2, axis=0, keepdims=True)
    B1[0, 2:3] = jnp.sum(n1 * n2, axis=0, keepdims=True)
    B1[0, 3:4] = jnp.zeros((1, COLS), F32)
    middle, last = exchange(net, me, B1, B2, merge_sums, merge_sums)
    correlate(me.z)
    for s in range(3):
        for half in (0, 1):
            for d in (1, -1):
                passed[s, d, half].wait_recv()
        pass_on(s + 1)
        for d in (1, -1):
            correlate(me.Z(-d * (s + 1)))
        if s == 0:
            columns = middle()
        if s == 1:
            sums = last(columns) / TOKENS
            D[...] = sums[2:3]
            E[0, 0:1] = sums[1:2]
            spread_out = [net.send(E.at[0], E.at[d], me.up(d)) for d in range(1, NZ)]
    passed[3, 1, 0].wait_recv()
    passed[3, -1, 1].wait_recv()
    correlate(me.Z(4))
    for copy, b in pairs:
        copy.wait_recv()
        pair_add(me, Pb, S, b)
    halves = scatter_plane(net, me, S, M1, F1, Q, M2, F2)
    own = me.block(0, 0)
    shape = (64, COLS)
    for o in (0, 1):
        crossed = halves[o] / TOKENS
        row = own * 128 + 64 * o + lax.broadcasted_iota(jnp.int32, shape, 0)
        column = me.z * COLS + lax.broadcasted_iota(jnp.int32, shape, 1)
        G[own, 64 * o : 64 * o + 64] = jnp.where(
            row == column, 2.0 * (D[...] - 1.0), 2.0 * offdiag_weight * crossed
        ).astype(BF)
    gather_plane(net, me, G)
    for copy in spread_out:
        copy.wait_recv()

    def means(value):
        high = value.astype(BF)
        low = (value - high.astype(F32)).astype(BF)
        rest = jnp.zeros((PAD - ROWS - 2, COLS), BF)
        return jnp.concatenate([high, low, rest], axis=0)

    N[ROWS:PAD] = means(sums[0:1])
    for d in range(NZ):
        A[me.Z(-d), ROWS:PAD] = means(E[d, 0:1])
    net.drain()


def upstream_kernel(A, N, G, D, normed, spread, down, T, R, U, V, Lo, Li, ssem, rsem):
    me = Place()
    barrier(me.z_peers())
    net = Net(ssem, rsem)
    ring = ScatterZ(net, me, T, R, ROWS)
    ones = jnp.ones((16, COLS), BF)
    diagonal = (D[...] - 1.0) * 2.0
    diagonal = diagonal.astype(BF).astype(F32) * D[...]
    levels = []

    def block(d):
        b = me.Z(d)
        g = G[pl.ds(4 * b, 4)].reshape(COLS, COLS)
        t = dot(N[...], g, ((1,), (1,)))
        squares = g * g
        if d == 0:
            shape = (COLS, COLS)
            same = lax.broadcasted_iota(jnp.int32, shape, 0) == lax.broadcasted_iota(
                jnp.int32, shape, 1
            )
            squares = jnp.where(same, 0.0, squares.astype(F32)).astype(BF)
            V[...] = t[0:ROWS]
        else:
            T[b] = t[0:ROWS].astype(BF)
        slope = dot(ones, squares, ((1,), (1,)))[0:1] * (0.5 / offdiag_weight)
        if d == 0:
            slope = slope + diagonal
        out = Li if d == 0 else Lo
        out[d, 0:1] = t[ROWS : ROWS + 1] + t[ROWS + 1 : ROWS + 2]
        out[d, 1:2] = slope
        if d != 0:
            levels.append(net.send(Lo.at[d], Li.at[d], me.up(d)))
        return g, b, squares

    def first_view(g, b, squares, start):
        u = dot(A[b], g, ((1,), (0,)))
        s = dot(ones, squares, ((1,), (0,)))[0:8]
        if start:
            U[0:PAD] = u
            U[PAD : PAD + 8] = s
        else:
            U[0:PAD] += u
            U[PAD : PAD + 8] += s

    four = block(4)
    ring.long(0)
    three = block(3), block(5)
    ring.short(1)
    first_view(*four, True)
    first_view(*three[0], False)
    first_view(*three[1], False)
    two = block(2), block(6)
    ring.long(1)
    ring.short(2)
    first_view(*two[0], False)
    first_view(*two[1], False)
    one = block(1), block(7)
    ring.long(2)
    ring.short(3)
    first_view(*one[0], False)
    first_view(*one[1], False)
    first_view(*block(0), False)
    ring.long(3)

    def finish(view, upstream, level, slope):
        n = normed[view].astype(F32)
        down[view] = ((upstream - level - n * slope) / spread[view : view + 1]).astype(BF)

    level = U[ROWS : ROWS + 1] + U[ROWS + 1 : ROWS + 2]
    slope = U[PAD : PAD + 1] * (0.5 / offdiag_weight) + diagonal
    finish(0, U[0:ROWS], level, slope)
    for copy in levels:
        copy.wait_recv()
    both = merge_sums(Li)
    second = jnp.concatenate([ring.finish(0), ring.finish(1)], axis=0) + V[...]
    finish(1, second, both[0:1], both[1:2])
    net.drain()


def grads_kernel(
    down, W, hf, hs, gw, gh, T, R, V, Pb, S, M1, F1, Q, M2, F2, ssem, rsem
):
    me = Place()
    barrier(me.plane_peers() + me.z_peers())
    net = Net(ssem, rsem)
    ring = ScatterZ(net, me, T, R, 2 * ROWS)
    both = down[...].reshape(2 * ROWS, COLS)

    def block(d):
        b = me.Z(d)
        w = W[pl.ds(4 * b, 4)].reshape(COLS, COLS)
        t = dot(down[...].reshape(2 * ROWS, COLS), w, ((1,), (1,)))
        if d == 0:
            V[...] = t
        else:
            T[b] = t.astype(BF)

    pairs = []

    def weight(b):
        cols = pl.ds(pl.multiple_of(b * COLS, COLS), COLS)
        t = dot(hf[:, cols], down[0], ((0,), (0,))) + dot(hs[:, cols], down[1], ((0,), (0,)))
        store_block(Pb, b, t)
        pairs.append((pair_send(net, me, Pb, S, b), b))

    block(4)
    ring.long(0)
    block(3)
    block(5)
    ring.short(1)
    for b in range(8):
        weight(jnp.int32(b))
    block(2)
    block(6)
    ring.long(1)
    block(1)
    block(7)
    block(0)
    for copy, b in pairs:
        copy.wait_recv()
        pair_add(me, Pb, S, b)
    ring.short(2)
    halves = scatter_plane(net, me, S, M1, F1, Q, M2, F2)
    for o in (0, 1):
        gw[64 * o : 64 * o + 64] = (halves[o] / math.sqrt(TOKENS)).astype(BF)
    ring.long(2)
    ring.short(3)
    ring.long(3)
    for half in (0, 1):
        rows = pl.ds(ROWS * half, ROWS)
        gh[half] = (ring.finish(half) + V[rows]).astype(BF)
    net.drain()


VM = pl.BlockSpec(memory_space=pltpu.VMEM)


def call(kernel, ident, outs, scratch, count, args):
    return pl.pallas_call(
        kernel,
        out_shape=[jax.ShapeDtypeStruct(s, t) for s, t in outs],
        in_specs=[VM] * len(args),
        out_specs=[VM] * len(outs),
        scratch_shapes=scratch
        + [pltpu.SemaphoreType.DMA((count,)), pltpu.SemaphoreType.DMA((count,))],
        compiler_params=pltpu.CompilerParams(
            collective_id=ident, has_side_effects=True, vmem_limit_bytes=56 * 1024 * 1024
        ),
    )(*args)


def local(hidden_first, hidden_second, weight):
    W, normed, spread = call(
        project_kernel,
        1,
        [((32, 128, COLS), BF), ((2, ROWS, COLS), BF), ((2, COLS), F32)],
        [
            pltpu.VMEM((2, ROWS, COLS), F32),
            pltpu.VMEM((8, 4, COLS), F32),
            pltpu.VMEM((4, 4, COLS), F32),
        ],
        96,
        (hidden_first, hidden_second, weight),
    )
    A, N, G, D = call(
        corr_kernel,
        2,
        [
            ((NZ, PAD, COLS), BF),
            ((PAD, COLS), BF),
            ((32, 128, COLS), BF),
            ((1, COLS), F32),
        ],
        [pltpu.VMEM((4, 4, 2, 128, COLS), BF), pltpu.VMEM((4, 4, 128, COLS), BF)]
        + scatter_plane_scratch()
        + [
            pltpu.VMEM((8, 4, COLS), F32),
            pltpu.VMEM((4, 4, COLS), F32),
            pltpu.VMEM((NZ, 1, COLS), F32),
        ],
        160,
        (normed,),
    )
    (down,) = call(
        upstream_kernel,
        3,
        [((2, ROWS, COLS), BF)],
        [
            pltpu.VMEM((NZ, ROWS, COLS), BF),
            pltpu.VMEM((2, 4, ROWS, COLS), BF),
            pltpu.VMEM((PAD + 8, COLS), F32),
            pltpu.VMEM((ROWS, COLS), F32),
            pltpu.VMEM((NZ, 2, COLS), F32),
            pltpu.VMEM((NZ, 2, COLS), F32),
        ],
        32,
        (A, N, G, D, normed, spread),
    )
    gw, gh = call(
        grads_kernel,
        4,
        [((128, COLS), BF), ((2, ROWS, COLS), BF)],
        [
            pltpu.VMEM((NZ, 2 * ROWS, COLS), BF),
            pltpu.VMEM((2, 4, 2 * ROWS, COLS), BF),
            pltpu.VMEM((2 * ROWS, COLS), F32),
            pltpu.VMEM((4, 4, 2, 128, COLS), BF),
            pltpu.VMEM((4, 4, 128, COLS), BF),
        ]
        + scatter_plane_scratch(),
        64,
        (down, W, hidden_first, hidden_second),
    )
    return gw, gh[0], gh[1]


def solution(mesh):
    in_specs = (P("dp", None), P("dp", None), P("dp", "mp"))
    out_specs = (P("dp", "mp"), P("dp", "mp"), P("dp", "mp"))
    return jax.shard_map(local, mesh=mesh, in_specs=in_specs, out_specs=out_specs, check_vma=False)
```

```python
import math

import jax
import jax.numpy as jnp
from jax import lax
from jax.experimental import pallas as pl
from jax.experimental.pallas import tpu as pltpu
from jax.sharding import PartitionSpec as P

MESH = pl.DeviceIdType.MESH
BF = jnp.bfloat16
F32 = jnp.float32

epsilon = 1e-05
offdiag_weight = 0.0051

TOKENS = 6144
ROWS = 192
PAD = 208
COLS = 512
NZ = 8
SLOTS = (0, 1, -1, 2, -2, 3, -3, 4)


def wrap(value, size):
    return lax.rem(value + size, size)


class Place:
    def __init__(self):
        dp = lax.axis_index("dp")
        self.dp = dp
        self.x = lax.div(dp, 8)
        self.y = lax.rem(lax.div(dp, 2), 4)
        self.c = lax.rem(dp, 2)
        self.z = lax.axis_index("mp")

    def X(self, d):
        return wrap(self.x + d, 4)

    def Y(self, d):
        return wrap(self.y + d, 4)

    def Z(self, d):
        return wrap(self.z + d, NZ)

    def block(self, dx, dy, dc=0):
        return self.X(dx) * 8 + self.Y(dy) * 2 + wrap(self.c + dc, 2)

    def at(self, dx, dy, dc=0):
        return {"dp": self.block(dx, dy, dc)}

    def sib(self):
        return {"dp": self.dp + 1 - 2 * self.c}

    def up(self, d):
        return {"mp": self.Z(d)}

    def plane_peers(self):
        row = [(0, dy, dc) for dy in range(4) for dc in range(2)][1:]
        column = [(dx, 0, 0) for dx in range(1, 4)]
        return [self.at(*p) for p in row + column]

    def z_peers(self):
        return [self.up(d) for d in range(1, NZ)]


class Net:
    def __init__(self, sends, recvs):
        self.sends, self.recvs = sends, recvs
        self.copies = []

    def send(self, src, dst, to):
        index = len(self.copies)
        copy = pltpu.make_async_remote_copy(
            src_ref=src,
            dst_ref=dst,
            send_sem=self.sends.at[index],
            recv_sem=self.recvs.at[index],
            device_id=to,
            device_id_type=MESH,
        )
        copy.start()
        self.copies.append(copy)
        return copy

    def drain(self):
        for copy in self.copies:
            copy.wait_send()


def barrier(peers):
    sem = pltpu.get_barrier_semaphore()
    for peer in peers:
        pl.semaphore_signal(sem, inc=1, device_id=peer, device_id_type=MESH)
    pl.semaphore_wait(sem, len(peers))


def dot(a, b, dims):
    return lax.dot_general(a, b, ((dims[0], dims[1]), ((), ())), preferred_element_type=F32)


def turn(o, first, second):
    return (first, second) if o == 0 else (second, first)


def finish(steps):
    for _ in steps:
        pass


def gather_plane(net, me, W):
    rows = W.shape[1]
    part, quarter = rows // 2, rows // 4

    def block(o, a, b):
        return me.block(*turn(o, a, b))

    def to(o, a, b):
        return me.at(*turn(o, a, b))

    def push(index, start, size, target):
        ref = W.at[index, pl.ds(start, size)]
        return net.send(ref, ref, target)

    own = me.block(0, 0)
    both = [(o, d) for d in (1, -1) for o in (0, 1)]
    first, second, far, sibs = {}, {}, {}, []

    def over(o, a):
        for d in (1, -1):
            second[o, a, d] = push(block(o, a, 0), part * o, part, to(o, 0, d))

    def share(o, a, b):
        sibs.append(push(block(o, a, b), part * o, part, me.sib()))

    for d in (1, -1, 2):
        for o in (0, 1):
            first[o, d] = push(own, part * o, part, to(o, d, 0))
    for o in (0, 1):
        over(o, 0)
    sibs.append(net.send(W.at[own], W.at[own], me.sib()))
    yield
    for d in (1, -1, 2):
        for o in (0, 1):
            first[o, d].wait_recv()
            over(o, -d)
        for o in (0, 1):
            share(o, -d, 0)
    yield
    for a in (0, -1, 1, -2):
        for o, d in both:
            second[o, a, d].wait_recv()
            far[o, a, d] = push(
                block(o, a, -d), part * o + (0 if d == 1 else quarter), quarter, to(o, 0, d)
            )
        for o, d in both:
            share(o, a, -d)
    yield
    for a in (0, -1, 1, -2):
        for o in (0, 1):
            far[o, a, 1].wait_recv()
            far[o, a, -1].wait_recv()
            share(o, a, 2)
    yield
    for copy in sibs:
        copy.wait_recv()


def scatter_plane(net, me, S, M1, F1, Q, F2, result):
    half_rows = S.shape[2] // 2

    def index(o, d):
        return me.X(d) if o == 0 else me.Y(d)

    def other(o, d):
        return me.Y(d) if o == 0 else me.X(d)

    def part(o, d, start, size=2):
        rows = pl.ds(half_rows * o, half_rows)
        if o == 0:
            return (index(o, d), pl.ds(start, size), rows)
        return (pl.ds(start, size), index(o, d), rows)

    def to(o, a, b):
        return me.at(*turn(o, a, b))

    both = [(o, d) for d in (1, -1) for o in (0, 1)]
    slot = {1: 0, -1: 1, 2: 2}
    mid, early, late, last = {}, {}, {}, {}
    for o, d in both:
        h = 0 if d == 1 else 2
        mid[o, d] = net.send(S.at[part(o, 2, h)], M1.at[o, slot[d]], to(o, d, 0))
    for o, d in both:
        h = 0 if d == 1 else 2
        early[o, d] = net.send(
            S.at[part(o, d, 2 - h)], F1.at[o, slot[d], pl.ds(2 - h, 2)], to(o, d, 0)
        )
    yield
    for o, d in both:
        h = 0 if d == 1 else 2
        mid[o, d].wait_recv()
        S[part(o, d, h)] += M1[o, slot[d]]
        late[o, d] = net.send(S.at[part(o, d, h)], F1.at[o, slot[d], pl.ds(h, 2)], to(o, d, 0))
    yield
    for o in (0, 1):
        for d in (1, -1):
            early[o, d].wait_recv()
            late[o, d].wait_recv()
        total = S[part(o, 0, 0, 4)].astype(F32) + F1[o, 0].astype(F32) + F1[o, 1].astype(F32)
        Q[o] = total.astype(BF)
        for d in (1, -1, 2):
            last[o, d] = net.send(Q.at[o, other(o, d)], F2.at[o, slot[d]], to(o, 0, d))
    yield
    for o in (0, 1):
        for d in (1, -1, 2):
            last[o, d].wait_recv()
        result.append(
            (Q[o, other(o, 0)].astype(F32) + F2[o, 0].astype(F32))
            + (F2[o, 1].astype(F32) + F2[o, 2].astype(F32))
        )


def scatter_plane_scratch(rows):
    return [
        pltpu.VMEM((4, 4, 2, rows, COLS), BF),
        pltpu.VMEM((4, 4, rows, COLS), BF),
        pltpu.VMEM((2, 2, 2, rows // 2, COLS), BF),
        pltpu.VMEM((2, 2, 4, rows // 2, COLS), BF),
        pltpu.VMEM((2, 4, rows // 2, COLS), BF),
        pltpu.VMEM((2, 3, rows // 2, COLS), BF),
    ]


class ScatterZ:
    def __init__(self, net, me, T, R, rows):
        self.net, self.me, self.T, self.R = net, me, T, R
        self.half = rows // 2
        self.copies = {}

    def slice(self, half):
        return pl.ds(half * self.half, self.half)

    def send(self, d, s, half):
        slot = 0 if d == 1 else 1
        index = self.me.Z(d * (4 - s))
        rows = self.slice(half)
        previous = self.copies.get((d, s - 1, half))
        if previous is not None:
            previous.wait_recv()
            self.T[index, rows] += self.R[slot, s - 1, rows]
        self.copies[d, s, half] = self.net.send(
            self.T.at[index, rows], self.R.at[slot, s, rows], self.me.up(d)
        )

    def long(self, s):
        self.send(1, s, 0)
        self.send(-1, s, 1)

    def short(self, s):
        self.send(1, s, 1)
        self.send(-1, s, 0)

    def finish(self, half):
        for d in (1, -1):
            self.copies[d, 3, half].wait_recv()
        rows = self.slice(half)
        return self.R[0, 3, rows].astype(F32) + self.R[1, 3, rows].astype(F32)


def exchange(net, me, B1, B2, merge1, merge2):
    copies = []
    for dy in range(4):
        for dc in range(2):
            if dy + dc > 0:
                copies.append(net.send(B1.at[0], B1.at[2 * dy + dc], me.at(0, dy, dc)))

    def middle():
        for copy in copies:
            copy.wait_recv()
        B2[0] = merge1(B1)
        return [net.send(B2.at[0], B2.at[dx], me.at(dx, 0, 0)) for dx in range(1, 4)]

    def last(second):
        for copy in second:
            copy.wait_recv()
        return merge2(B2)

    return middle, last


def merge_moments(rows):
    def merge(B):
        count = B.shape[0]
        result = []
        for view in range(2):
            means = [B[k, 2 * view : 2 * view + 1] for k in range(count)]
            squares = [B[k, 2 * view + 1 : 2 * view + 2] for k in range(count)]
            mean = sum(means) / count
            square = sum(squares) + rows * sum((m - mean) * (m - mean) for m in means)
            result += [mean, square]
        return jnp.concatenate(result, axis=0)

    return merge


def merge_sums(B):
    return sum(B[k] for k in range(B.shape[0]))


class Pairs:
    def __init__(self, net, me, Pb, S):
        self.net, self.me, self.Pb, self.S = net, me, Pb, S
        self.copies = []

    def put(self, slot, value):
        rows = pl.ds(16 * slot, 16)
        self.Pb[:, :, :, rows] = value.astype(BF).reshape(4, 4, 2, 16, COLS)
        copy = self.net.send(
            self.Pb.at[:, :, 1 - self.me.c, rows], self.S.at[:, :, rows], self.me.sib()
        )
        self.copies.append((copy, slot))

    def add(self):
        for copy, slot in self.copies:
            rows = pl.ds(16 * slot, 16)
            copy.wait_recv()
            self.S[:, :, rows] += self.Pb[:, :, self.me.c, rows]


class Blocks:
    def __init__(self, net, me, Pb, S):
        self.net, self.me, self.Pb, self.S = net, me, Pb, S
        self.copies = []

    def where(self, b):
        return (b // 2, pl.ds(2 * (b % 2), 2))

    def put(self, b, value):
        where = self.where(b)
        self.Pb[where] = value.astype(BF).reshape(2, 2, 128, COLS)
        copy = self.net.send(
            self.Pb.at[where + (1 - self.me.c,)], self.S.at[where], self.me.sib()
        )
        self.copies.append((copy, where))

    def add(self):
        for copy, where in self.copies:
            copy.wait_recv()
            self.S[where] += self.Pb[where + (self.me.c,)]


class GatherZ:
    def __init__(self, net, me, A):
        self.net, self.me, self.A = net, me, A
        self.copies = {}

    def send(self, s, d, half):
        ref = self.A.at[self.me.Z(-d * s), pl.ds(96 * half, 96)]
        self.copies[s, d, half] = self.net.send(ref, ref, self.me.up(d))

    def start(self):
        for turn_ in (0, 1):
            for d in (1, -1):
                self.send(0, d, turn_ if d == 1 else 1 - turn_)

    def step(self, s):
        for turn_ in (0, 1):
            for d in (1, -1):
                half = turn_ if d == 1 else 1 - turn_
                if (s, d, half) in self.copies:
                    self.copies[s, d, half].wait_recv()
                    if s < 2 or (s == 2 and turn_ == 0):
                        self.send(s + 1, d, half)


def means(value):
    high = value.astype(BF)
    low = (value - high.astype(F32)).astype(BF)
    rest = jnp.zeros((PAD - ROWS - 2, COLS), BF)
    return jnp.concatenate([high, low, rest], axis=0)


def kernel(
    hf, hs, w, gw, g1, g2,
    H, W, acc, DN, A1, A2, X1, X2, Y1, Y2, E, GA, GB, G2, U, T1, R1, T2, R2, V1, V2,
    PA, SA, MA, FA, QA, LA, PB, SB, MB, FB, QB, LB, PG, SG, MG, FG, QG, LG,
    lsem, ssem, rsem,
):
    me = Place()
    net = Net(ssem, rsem)
    own = me.block(0, 0)
    loads = [
        pltpu.make_async_copy(w, W.at[own], lsem.at[0]),
        pltpu.make_async_copy(hf, H.at[pl.ds(0, ROWS)], lsem.at[1]),
        pltpu.make_async_copy(hs, H.at[pl.ds(ROWS, ROWS)], lsem.at[2]),
    ]
    for load in loads:
        load.start()
    barrier(me.plane_peers() + me.z_peers())
    loads[0].wait()
    finish(gather_plane(net, me, W))
    loads[1].wait()
    loads[2].wait()

    acc[...] = jnp.zeros_like(acc)

    def project(k, _):
        cols = pl.ds(pl.multiple_of(k * 1024, 1024), 1024)
        piece = W[pl.ds(8 * k, 8)].reshape(1024, COLS)
        acc[...] += jnp.dot(H[:, cols], piece, preferred_element_type=F32)
        return 0

    lax.fori_loop(0, 4, project, 0)

    def view(v):
        return slice(v * ROWS, (v + 1) * ROWS)

    for v in range(2):
        mean = jnp.sum(acc[view(v)], axis=0, keepdims=True) / ROWS
        shifted = acc[view(v)] - mean
        X1[0, 2 * v : 2 * v + 1] = mean
        X1[0, 2 * v + 1 : 2 * v + 2] = jnp.sum(shifted * shifted, axis=0, keepdims=True)
    middle, last = exchange(net, me, X1, X2, merge_moments(ROWS), merge_moments(8 * ROWS))
    moments = last(middle())
    spread = []
    for v, A in ((0, A1), (1, A2)):
        mean = moments[2 * v : 2 * v + 1]
        spread.append(jnp.sqrt(moments[2 * v + 1 : 2 * v + 2] / TOKENS + epsilon))
        A[me.z, 0:ROWS] = ((acc[view(v)] - mean) / spread[v]).astype(BF)

    gz2 = GatherZ(net, me, A2)
    gz1 = GatherZ(net, me, A1)
    gz2.start()
    n1, n2 = A1[me.z, 0:ROWS].astype(F32), A2[me.z, 0:ROWS].astype(F32)
    Y1[0, 0:1] = jnp.sum(n1, axis=0, keepdims=True)
    Y1[0, 1:2] = jnp.sum(n2, axis=0, keepdims=True)
    Y1[0, 2:3] = jnp.sum(n1 * n2, axis=0, keepdims=True)
    Y1[0, 3:4] = jnp.zeros((1, COLS), F32)
    middle, last = exchange(net, me, Y1, Y2, merge_sums, merge_sums)
    groups = (Pairs(net, me, PA, SA), Pairs(net, me, PB, SB))

    def correlate(slot):
        value = dot(A2[me.Z(SLOTS[slot]), 0:ROWS], A1[me.z, 0:ROWS], ((0,), (0,)))
        groups[slot // 4].put(slot % 4, value)

    halves_a, halves_b = [], []
    scatter_a = scatter_plane(net, me, SA, MA, FA, QA, LA, halves_a)
    scatter_b = scatter_plane(net, me, SB, MB, FB, QB, LB, halves_b)
    correlate(0)
    gz2.step(0)
    correlate(1)
    correlate(2)
    columns = middle()
    gz2.step(1)
    correlate(3)
    groups[0].add()
    next(scatter_a)
    correlate(4)
    sums = last(columns) / TOKENS
    E[0, 0:2] = sums[0:2]
    tops = [net.send(E.at[0], E.at[d], me.up(d)) for d in range(1, NZ)]
    gz2.step(2)
    correlate(5)
    correlate(6)
    next(scatter_a)
    gz2.step(3)
    gz1.start()
    correlate(7)
    groups[1].add()
    next(scatter_b)
    next(scatter_a)
    next(scatter_b)

    diagonal = 2.0 * (sums[2:3] - 1.0)

    def loss_grad(G, halves, group):
        for o in (0, 1):
            rows = pl.ds(32 * o, 32)
            value = (2.0 * offdiag_weight / TOKENS) * halves[o]
            if group == 0 and o == 0:
                row = lax.broadcasted_iota(jnp.int32, (32, COLS), 0)
                column = lax.broadcasted_iota(jnp.int32, (32, COLS), 1)
                same = jnp.logical_and(row < 16, row + 16 * own == column)
                value = jnp.where(same, diagonal, value)
            G[own, rows] = value.astype(BF)

    across = []

    def turn_over(G, group):
        for k in range(4):
            slot = 4 * group + k
            offset = SLOTS[slot]
            source = G.at[own, pl.ds(16 * k, 16)]
            if offset == 0:
                G2[own, 0:16] = G[own, 0:16]
            else:
                there = 7 if offset == 4 else SLOTS.index(-offset)
                across.append(
                    net.send(source, G2.at[own, pl.ds(16 * there, 16)], me.up(offset))
                )

    finish(scatter_a)
    loss_grad(GA, halves_a, 0)
    gather_a = gather_plane(net, me, GA)
    next(gather_a)
    turn_over(GA, 0)
    next(scatter_b)
    gz1.step(0)
    next(gather_a)
    finish(scatter_b)
    loss_grad(GB, halves_b, 1)
    gather_b = gather_plane(net, me, GB)
    next(gather_b)
    turn_over(GB, 1)
    next(gather_a)
    next(gather_b)
    next(gather_a)
    gz1.step(1)
    for copy in tops:
        copy.wait_recv()
    for d in range(NZ):
        A1[me.Z(-d), ROWS:PAD] = means(E[d, 0:1])
        A2[me.Z(-d), ROWS:PAD] = means(E[d, 1:2])
    next(gather_b)
    finish(gather_a)
    ones = jnp.ones((16, COLS), BF)

    def upstream(A, G, slot, dims, start):
        rows = pl.ds(16 * (slot % (G.shape[1] // 16)), 16)
        g = G[:, rows].reshape(COLS, COLS)
        squares = g * g
        if slot == 0:
            shape = (COLS, COLS)
            same = lax.broadcasted_iota(jnp.int32, shape, 0) == lax.broadcasted_iota(
                jnp.int32, shape, 1
            )
            squares = jnp.where(same, 0.0, squares.astype(F32)).astype(BF)
        u = dot(A[me.Z(SLOTS[slot])], g, ((1,), dims))
        s = dot(ones, squares, ((1,), dims))[0:8]
        if start:
            U[0:PAD] = u
            U[PAD : PAD + 8] = s
        else:
            U[0:PAD] += u
            U[PAD : PAD + 8] += s

    own_slope = diagonal.astype(BF).astype(F32) * sums[2:3]

    def down(v, A):
        level = U[ROWS : ROWS + 1] + U[ROWS + 1 : ROWS + 2]
        slope = U[PAD : PAD + 1] * (0.5 / offdiag_weight) + own_slope
        n = A[me.z, 0:ROWS].astype(F32)
        DN[view(v)] = ((U[0:ROWS] - level - n * slope) / spread[v]).astype(BF)

    def partial(v, T, V, d):
        b = me.Z(d)
        piece = W[pl.ds(4 * b, 4)].reshape(COLS, COLS)
        t = dot(DN[view(v)], piece, ((1,), (1,)))
        if d == 0:
            V[...] = t
        else:
            T[b] = t.astype(BF)

    for slot in range(4):
        upstream(A2, GA, slot, (0,), slot == 0)
    next(gather_b)
    gz1.step(2)
    for copy in across:
        copy.wait_recv()
    gather_2 = gather_plane(net, me, G2)
    next(gather_2)
    finish(gather_b)
    for slot in range(4, 8):
        upstream(A2, GB, slot, (0,), False)
    down(0, A1)
    ring1 = ScatterZ(net, me, T1, R1, ROWS)
    ring2 = ScatterZ(net, me, T2, R2, ROWS)
    gz1.step(3)
    partial(0, T1, V1, 4)
    ring1.long(0)
    partial(0, T1, V1, 3)
    partial(0, T1, V1, -3)
    ring1.short(1)
    next(gather_2)
    partial(0, T1, V1, 2)
    partial(0, T1, V1, -2)
    ring1.long(1)
    ring1.short(2)
    partial(0, T1, V1, 1)
    partial(0, T1, V1, -1)
    next(gather_2)
    ring1.long(2)
    ring1.short(3)
    partial(0, T1, V1, 0)
    next(gather_2)
    ring1.long(3)
    finish(gather_2)
    for slot in range(8):
        upstream(A1, G2, slot, (1,), slot == 0)
    down(1, A2)
    partial(1, T2, V2, 4)
    ring2.long(0)
    partial(1, T2, V2, 3)
    partial(1, T2, V2, -3)
    ring2.short(1)
    weight = Blocks(net, me, PG, SG)
    for b in range(8):
        cols = pl.ds(b * COLS, COLS)
        weight.put(b, dot(H[:, cols], DN[...], ((0,), (0,))))
    partial(1, T2, V2, 2)
    partial(1, T2, V2, -2)
    ring2.long(1)
    partial(1, T2, V2, 1)
    partial(1, T2, V2, -1)
    ring2.short(2)
    halves_g = []
    scatter_g = scatter_plane(net, me, SG, MG, FG, QG, LG, halves_g)
    weight.add()
    next(scatter_g)
    ring2.long(2)
    next(scatter_g)
    ring2.short(3)
    partial(1, T2, V2, 0)
    next(scatter_g)
    ring2.long(3)
    for ring, V, out in ((ring1, V1, g1), (ring2, V2, g2)):
        for half in (0, 1):
            rows = pl.ds(96 * half, 96)
            out[rows] = (ring.finish(half) + V[rows]).astype(BF)
    finish(scatter_g)
    for o in (0, 1):
        gw[64 * o : 64 * o + 64] = (halves_g[o] / math.sqrt(TOKENS)).astype(BF)
    net.drain()


def local(hidden_first, hidden_second, weight):
    vm = pl.BlockSpec(memory_space=pltpu.VMEM)
    hbm = pl.BlockSpec(memory_space=pl.ANY)
    count = 640
    return pl.pallas_call(
        kernel,
        out_shape=[
            jax.ShapeDtypeStruct((128, COLS), BF),
            jax.ShapeDtypeStruct((ROWS, COLS), BF),
            jax.ShapeDtypeStruct((ROWS, COLS), BF),
        ],
        in_specs=[hbm] * 3,
        out_specs=[vm] * 3,
        scratch_shapes=[
            pltpu.VMEM((2 * ROWS, 4096), BF),
            pltpu.VMEM((32, 128, COLS), BF),
            pltpu.VMEM((2 * ROWS, COLS), F32),
            pltpu.VMEM((2 * ROWS, COLS), BF),
            pltpu.VMEM((NZ, PAD, COLS), BF),
            pltpu.VMEM((NZ, PAD, COLS), BF),
            pltpu.VMEM((8, 4, COLS), F32),
            pltpu.VMEM((4, 4, COLS), F32),
            pltpu.VMEM((8, 4, COLS), F32),
            pltpu.VMEM((4, 4, COLS), F32),
            pltpu.VMEM((NZ, 2, COLS), F32),
            pltpu.VMEM((32, 64, COLS), BF),
            pltpu.VMEM((32, 64, COLS), BF),
            pltpu.VMEM((32, 128, COLS), BF),
            pltpu.VMEM((PAD + 8, COLS), F32),
            pltpu.VMEM((NZ, ROWS, COLS), BF),
            pltpu.VMEM((2, 4, ROWS, COLS), BF),
            pltpu.VMEM((NZ, ROWS, COLS), BF),
            pltpu.VMEM((2, 4, ROWS, COLS), BF),
            pltpu.VMEM((ROWS, COLS), F32),
            pltpu.VMEM((ROWS, COLS), F32),
        ]
        + scatter_plane_scratch(64)
        + scatter_plane_scratch(64)
        + scatter_plane_scratch(128)
        + [
            pltpu.SemaphoreType.DMA((3,)),
            pltpu.SemaphoreType.DMA((count,)),
            pltpu.SemaphoreType.DMA((count,)),
        ],
        compiler_params=pltpu.CompilerParams(
            collective_id=1, has_side_effects=True, vmem_limit_bytes=60 * 1024 * 1024
        ),
    )(hidden_first, hidden_second, weight)


def solution(mesh):
    in_specs = (P("dp", None), P("dp", None), P("dp", "mp"))
    out_specs = (P("dp", "mp"), P("dp", "mp"), P("dp", "mp"))
    return jax.shard_map(local, mesh=mesh, in_specs=in_specs, out_specs=out_specs, check_vma=False)
```

```python
import math

import jax
import jax.numpy as jnp
from jax import lax
from jax.experimental import pallas as pl
from jax.experimental.pallas import tpu as pltpu
from jax.sharding import PartitionSpec as P

MESH = pl.DeviceIdType.MESH
BF = jnp.bfloat16
F32 = jnp.float32

epsilon = 1e-05
offdiag_weight = 0.0051

TOKENS = 6144
ROWS = 192
PAD = 208
COLS = 512
NZ = 8
SLOTS = (0, 1, -1, 2, -2, 3, -3, 4)


def wrap(value, size):
    return lax.rem(value + size, size)


class Place:
    def __init__(self):
        dp = lax.axis_index("dp")
        self.dp = dp
        self.x = lax.div(dp, 8)
        self.y = lax.rem(lax.div(dp, 2), 4)
        self.c = lax.rem(dp, 2)
        self.z = lax.axis_index("mp")

    def X(self, d):
        return wrap(self.x + d, 4)

    def Y(self, d):
        return wrap(self.y + d, 4)

    def Z(self, d):
        return wrap(self.z + d, NZ)

    def block(self, dx, dy, dc=0):
        return self.X(dx) * 8 + self.Y(dy) * 2 + wrap(self.c + dc, 2)

    def chip(self, dx, dy):
        return self.X(dx) * 4 + self.Y(dy)

    def at(self, dx, dy, dc=0):
        return {"dp": self.block(dx, dy, dc)}

    def sib(self):
        return {"dp": self.dp + 1 - 2 * self.c}

    def up(self, d):
        return {"mp": self.Z(d)}

    def plane_peers(self):
        row = [(0, dy, dc) for dy in range(4) for dc in range(2)][1:]
        column = [(dx, 0, 0) for dx in range(1, 4)]
        return [self.at(*p) for p in row + column]

    def z_peers(self):
        return [self.up(d) for d in range(1, NZ)]


class Net:
    def __init__(self, me, sent, recvs):
        self.me, self.sent, self.recvs = me, sent, recvs
        self.count = 0
        self.totals = []

    def group(self):
        self.count += 1
        return self.count - 1

    def sender(self, total):
        self.totals.append(total)
        return len(self.totals) - 1

    def copy(self, src, dst, to, sender, group):
        return pltpu.make_async_remote_copy(
            src_ref=src,
            dst_ref=dst,
            send_sem=self.sent.at[sender],
            recv_sem=self.recvs.at[group],
            device_id=to,
            device_id_type=MESH,
        )

    def send(self, src, dst, to, sender, group=None):
        copy = self.copy(src, dst, to, sender, self.group() if group is None else group)
        copy.start()
        return copy

    def wait(self, group, total):
        self.copy(total, total, self.me.sib(), 0, group).wait_recv()

    def drain(self):
        for sender, total in enumerate(self.totals):
            self.copy(total, total, self.me.sib(), sender, 0).wait_send()


def barrier(peers):
    sem = pltpu.get_barrier_semaphore()
    for peer in peers:
        pl.semaphore_signal(sem, inc=1, device_id=peer, device_id_type=MESH)
    pl.semaphore_wait(sem, len(peers))


def dot(a, b, dims):
    return lax.dot_general(a, b, ((dims[0], dims[1]), ((), ())), preferred_element_type=F32)


def turn(o, first, second):
    return (first, second) if o == 0 else (second, first)


def finish(steps):
    for _ in steps:
        pass


def gather_plane(net, me, W):
    rows = W.shape[2]
    part, quarter = rows // 2, rows // 4

    def block(o, a, b):
        return me.chip(*turn(o, a, b))

    def to(o, a, b):
        return me.at(*turn(o, a, b))

    def push(index, start, size, target, group=None):
        ref = W.at[index, me.c, pl.ds(start, size)]
        return net.send(ref, ref, target, many, group)

    own = me.chip(0, 0)
    block_ref = W.at[own, me.c]
    both = [(o, d) for d in (1, -1) for o in (0, 1)]
    first, second = {}, {}
    shared, far = net.group(), [net.group() for _ in range(4)]
    many, one = net.sender(W.at[pl.ds(0, 15)]), net.sender(block_ref)

    def over(o, a):
        for d in (1, -1):
            second[o, a, d] = push(block(o, a, 0), part * o, part, to(o, 0, d))

    def share(o, a, b):
        push(block(o, a, b), part * o, part, me.sib(), shared)

    for d in (1, -1, 2):
        for o in (0, 1):
            first[o, d] = push(own, part * o, part, to(o, d, 0))
    for o in (0, 1):
        over(o, 0)
    net.send(block_ref, block_ref, me.sib(), one, shared)
    yield
    for d in (1, -1, 2):
        for o in (0, 1):
            first[o, d].wait_recv()
            over(o, -d)
        for o in (0, 1):
            share(o, -d, 0)
    yield
    for k, a in enumerate((0, -1, 1, -2)):
        for o, d in both:
            second[o, a, d].wait_recv()
            start = part * o + (0 if d == 1 else quarter)
            push(block(o, a, -d), start, quarter, to(o, 0, d), far[k])
        for o, d in both:
            share(o, a, -d)
    yield
    for k, a in enumerate((0, -1, 1, -2)):
        net.wait(far[k], block_ref)
        for o in (0, 1):
            share(o, a, 2)
    yield
    net.wait(shared, W.at[:, 1 - me.c])


def scatter_plane(net, me, S, M1, F1, Q, F2, result):
    half_rows = S.shape[2] // 2

    def index(o, d):
        return me.X(d) if o == 0 else me.Y(d)

    def other(o, d):
        return me.Y(d) if o == 0 else me.X(d)

    def part(o, d, start, size=2):
        rows = pl.ds(half_rows * o, half_rows)
        if o == 0:
            return (index(o, d), pl.ds(start, size), rows)
        return (pl.ds(start, size), index(o, d), rows)

    def to(o, a, b):
        return me.at(*turn(o, a, b))

    both = [(o, d) for d in (1, -1) for o in (0, 1)]
    slot = {1: 0, -1: 1, 2: 2}
    mid = {}
    many, few = net.sender(S.at[pl.ds(0, 3)]), net.sender(F2)
    parts = [net.group() for _ in (0, 1)]
    ends = [net.group() for _ in (0, 1)]
    for o, d in both:
        h = 0 if d == 1 else 2
        mid[o, d] = net.send(S.at[part(o, 2, h)], M1.at[o, slot[d]], to(o, d, 0), many)
    for o, d in both:
        h = 0 if d == 1 else 2
        there = F1.at[o, slot[d], pl.ds(2 - h, 2)]
        net.send(S.at[part(o, d, 2 - h)], there, to(o, d, 0), many, parts[o])
    yield
    for o, d in both:
        h = 0 if d == 1 else 2
        mid[o, d].wait_recv()
        S[part(o, d, h)] += M1[o, slot[d]]
        there = F1.at[o, slot[d], pl.ds(h, 2)]
        net.send(S.at[part(o, d, h)], there, to(o, d, 0), many, parts[o])
    yield
    for o in (0, 1):
        net.wait(parts[o], F1.at[o])
        total = S[part(o, 0, 0, 4)].astype(F32) + F1[o, 0].astype(F32) + F1[o, 1].astype(F32)
        Q[o] = total.astype(BF)
        for d in (1, -1, 2):
            net.send(Q.at[o, other(o, d)], F2.at[o, slot[d]], to(o, 0, d), few, ends[o])
    yield
    for o in (0, 1):
        net.wait(ends[o], F2.at[o])
        result.append(
            (Q[o, other(o, 0)].astype(F32) + F2[o, 0].astype(F32))
            + (F2[o, 1].astype(F32) + F2[o, 2].astype(F32))
        )


def scatter_plane_scratch(rows):
    return [
        pltpu.VMEM((4, 4, 2, rows, COLS), BF),
        pltpu.VMEM((4, 4, rows, COLS), BF),
        pltpu.VMEM((2, 2, 2, rows // 2, COLS), BF),
        pltpu.VMEM((2, 2, 4, rows // 2, COLS), BF),
        pltpu.VMEM((2, 4, rows // 2, COLS), BF),
        pltpu.VMEM((2, 3, rows // 2, COLS), BF),
    ]


class ScatterZ:
    def __init__(self, net, me, T, R):
        self.net, self.me, self.T, self.R = net, me, T, R
        self.sender = net.sender(T.at[pl.ds(0, NZ - 1)])
        self.copies = {}

    def send(self, d, s, piece):
        slot = 0 if d == 1 else 1
        index = self.me.Z(d * (4 - s))
        rows = pl.ds(48 * piece, 48)
        previous = self.copies.get((d, s - 1, piece))
        if previous is not None:
            previous.wait_recv()
            self.T[index, rows] += self.R[slot, s - 1, rows]
        self.copies[d, s, piece] = self.net.send(
            self.T.at[index, rows], self.R.at[slot, s, rows], self.me.up(d), self.sender
        )

    def long(self, s):
        for i in (0, 1):
            self.send(1, s, i)
            self.send(-1, s, 2 + i)

    def short(self, s):
        for i in (0, 1):
            self.send(1, s, 2 + i)
            self.send(-1, s, i)

    def finish(self, V, write):
        for piece in (2, 0, 3, 1):
            rows = pl.ds(48 * piece, 48)
            for d in (1, -1):
                self.copies[d, 3, piece].wait_recv()
            write(
                48 * piece,
                V[rows] + (self.R[0, 3, rows].astype(F32) + self.R[1, 3, rows].astype(F32)),
            )


def exchange(net, me, B1, B2, merge1, merge2):
    row, column = B1.at[pl.ds(1, 7)], B2.at[pl.ds(1, 3)]
    one, two = net.group(), net.group()
    by = net.sender(row), net.sender(column)
    for dy in range(4):
        for dc in range(2):
            if dy + dc > 0:
                net.send(B1.at[0], B1.at[2 * dy + dc], me.at(0, dy, dc), by[0], one)

    def middle():
        net.wait(one, row)
        B2[0] = merge1(B1)
        for dx in range(1, 4):
            net.send(B2.at[0], B2.at[dx], me.at(dx, 0, 0), by[1], two)

    def last():
        net.wait(two, column)
        return merge2(B2)

    return middle, last


def merge_moments(rows):
    def merge(B):
        count = B.shape[0]
        result = []
        for view in range(2):
            means = [B[k, 2 * view : 2 * view + 1] for k in range(count)]
            squares = [B[k, 2 * view + 1 : 2 * view + 2] for k in range(count)]
            mean = sum(means) / count
            square = sum(squares) + rows * sum((m - mean) * (m - mean) for m in means)
            result += [mean, square]
        return jnp.concatenate(result, axis=0)

    return merge


def merge_sums(B):
    return sum(B[k] for k in range(B.shape[0]))


class Pairs:
    def __init__(self, net, me, Pb, S):
        self.net, self.me, self.Pb, self.S = net, me, Pb, S
        self.group, self.sender = net.group(), net.sender(S)
        self.places = []

    def put(self, slot, value):
        rows = pl.ds(16 * slot, 16)
        self.Pb[:, :, :, rows] = value.astype(BF).reshape(4, 4, 2, 16, COLS)
        there = self.S.at[:, :, rows]
        other = self.Pb.at[:, :, 1 - self.me.c, rows]
        self.net.send(other, there, self.me.sib(), self.sender, self.group)
        self.places.append(slot)

    def add(self):
        self.net.wait(self.group, self.S)
        for slot in self.places:
            rows = pl.ds(16 * slot, 16)
            self.S[:, :, rows] += self.Pb[:, :, self.me.c, rows]


class Blocks:
    def __init__(self, net, me, Pb, S):
        self.net, self.me, self.Pb, self.S = net, me, Pb, S
        self.group, self.sender = net.group(), net.sender(S)
        self.places = []

    def where(self, b):
        return (b // 2, pl.ds(2 * (b % 2), 2))

    def put(self, b, value):
        where = self.where(b)
        self.Pb[where] = value.astype(BF).reshape(2, 2, 128, COLS)
        other = self.Pb.at[where + (1 - self.me.c,)]
        self.net.send(other, self.S.at[where], self.me.sib(), self.sender, self.group)
        self.places.append(where)

    def add(self):
        self.net.wait(self.group, self.S)
        for where in self.places:
            self.S[where] += self.Pb[where + (self.me.c,)]


class GatherZ:
    def __init__(self, net, me, A):
        self.net, self.me, self.A = net, me, A
        self.sender = net.sender(A.at[pl.ds(0, NZ - 1), pl.ds(0, ROWS)])
        self.copies = {}

    def order(self):
        return [(1, 0), (-1, 2), (1, 1), (-1, 3), (1, 2), (-1, 0), (1, 3), (-1, 1)]

    def send(self, s, d, piece):
        ref = self.A.at[self.me.Z(-d * s), pl.ds(48 * piece, 48)]
        self.copies[s, d, piece] = self.net.send(ref, ref, self.me.up(d), self.sender)

    def start(self):
        for d, piece in self.order():
            self.send(0, d, piece)

    def step(self, s):
        for place, (d, piece) in enumerate(self.order()):
            if (s, d, piece) in self.copies:
                self.copies[s, d, piece].wait_recv()
                if s < 2 or (s == 2 and place < 4):
                    self.send(s + 1, d, piece)


def means(value):
    high = value.astype(BF)
    low = (value - high.astype(F32)).astype(BF)
    rest = jnp.zeros((PAD - ROWS - 2, COLS), BF)
    return jnp.concatenate([high, low, rest], axis=0)


def kernel(
    hf, hs, w, out,
    H, W, acc, DN, A1, A2, X1, X2, Y1, Y2, E, GA, GB, G2, U, T1, R1, T2, R2, V1, V2,
    PA, SA, MA, FA, QA, LA, PB, SB, MB, FB, QB, LB, PG, SG, MG, FG, QG, LG,
    lsem, ssem, rsem,
):
    me = Place()
    net = Net(me, ssem, rsem)
    own = me.block(0, 0)
    mine = (me.chip(0, 0), me.c)
    loads = [
        pltpu.make_async_copy(w, W.at[mine], lsem.at[0]),
        pltpu.make_async_copy(hf, H.at[pl.ds(0, ROWS)], lsem.at[1]),
        pltpu.make_async_copy(hs, H.at[pl.ds(ROWS, ROWS)], lsem.at[2]),
    ]
    for load in loads:
        load.start()
    barrier(me.plane_peers() + me.z_peers())
    loads[0].wait()
    finish(gather_plane(net, me, W))
    loads[1].wait()
    loads[2].wait()

    acc[...] = jnp.zeros_like(acc)

    def project(k, _):
        cols = pl.ds(pl.multiple_of(k * 1024, 1024), 1024)
        piece = W[pl.ds(4 * k, 4)].reshape(1024, COLS)
        acc[...] += jnp.dot(H[:, cols], piece, preferred_element_type=F32)
        return 0

    lax.fori_loop(0, 4, project, 0)

    def view(v):
        return slice(v * ROWS, (v + 1) * ROWS)

    for v in range(2):
        mean = jnp.sum(acc[view(v)], axis=0, keepdims=True) / ROWS
        shifted = acc[view(v)] - mean
        X1[0, 2 * v : 2 * v + 1] = mean
        X1[0, 2 * v + 1 : 2 * v + 2] = jnp.sum(shifted * shifted, axis=0, keepdims=True)
    middle, last = exchange(net, me, X1, X2, merge_moments(ROWS), merge_moments(8 * ROWS))
    middle()
    moments = last()
    spread = []
    for v, A in ((0, A1), (1, A2)):
        mean = moments[2 * v : 2 * v + 1]
        spread.append(jnp.sqrt(moments[2 * v + 1 : 2 * v + 2] / TOKENS + epsilon))
        A[me.z, 0:ROWS] = ((acc[view(v)] - mean) / spread[v]).astype(BF)

    gz2 = GatherZ(net, me, A2)
    gz1 = GatherZ(net, me, A1)
    gz2.start()
    n1, n2 = A1[me.z, 0:ROWS].astype(F32), A2[me.z, 0:ROWS].astype(F32)
    Y1[0, 0:1] = jnp.sum(n1, axis=0, keepdims=True)
    Y1[0, 1:2] = jnp.sum(n2, axis=0, keepdims=True)
    Y1[0, 2:3] = jnp.sum(n1 * n2, axis=0, keepdims=True)
    Y1[0, 3:4] = jnp.zeros((1, COLS), F32)
    middle, last = exchange(net, me, Y1, Y2, merge_sums, merge_sums)
    groups = (Pairs(net, me, PA, SA), Pairs(net, me, PB, SB))

    def correlate(slot):
        value = dot(A2[me.Z(SLOTS[slot]), 0:ROWS], A1[me.z, 0:ROWS], ((0,), (0,)))
        groups[slot // 4].put(slot % 4, value)

    halves_a, halves_b = [], []
    scatter_a = scatter_plane(net, me, SA, MA, FA, QA, LA, halves_a)
    scatter_b = scatter_plane(net, me, SB, MB, FB, QB, LB, halves_b)
    correlate(0)
    gz2.step(0)
    correlate(1)
    correlate(2)
    middle()
    gz2.step(1)
    correlate(3)
    groups[0].add()
    next(scatter_a)
    correlate(4)
    sums = last() / TOKENS
    E[0, 0:2] = sums[0:2]
    heads = net.group()
    heads_by = net.sender(E.at[pl.ds(1, NZ - 1)])
    for d in range(1, NZ):
        net.send(E.at[0], E.at[d], me.up(d), heads_by, heads)
    gz2.step(2)
    correlate(5)
    correlate(6)
    next(scatter_a)
    gz2.step(3)
    gz1.start()
    correlate(7)
    groups[1].add()
    next(scatter_b)
    next(scatter_a)
    next(scatter_b)

    diagonal = 2.0 * (sums[2:3] - 1.0)

    def loss_grad(G, halves, group):
        for o in (0, 1):
            rows = pl.ds(32 * o, 32)
            value = (2.0 * offdiag_weight / TOKENS) * halves[o]
            if group == 0 and o == 0:
                row = lax.broadcasted_iota(jnp.int32, (32, COLS), 0)
                column = lax.broadcasted_iota(jnp.int32, (32, COLS), 1)
                same = jnp.logical_and(row < 16, row + 16 * own == column)
                value = jnp.where(same, diagonal, value)
            G[mine + (rows,)] = value.astype(BF)

    turned_ref = G2.at[mine + (pl.ds(0, 112),)]
    turned, turned_by = net.group(), net.sender(turned_ref)

    def turn_over(G, group):
        for k in range(4):
            slot = 4 * group + k
            offset = SLOTS[slot]
            source = G.at[mine + (pl.ds(16 * k, 16),)]
            if offset == 0:
                G2[mine + (pl.ds(0, 16),)] = G[mine + (pl.ds(0, 16),)]
            else:
                there = 7 if offset == 4 else SLOTS.index(-offset)
                target = G2.at[mine + (pl.ds(16 * there, 16),)]
                net.send(source, target, me.up(offset), turned_by, turned)

    finish(scatter_a)
    loss_grad(GA, halves_a, 0)
    gather_a = gather_plane(net, me, GA)
    next(gather_a)
    turn_over(GA, 0)
    next(scatter_b)
    next(gather_a)
    finish(scatter_b)
    loss_grad(GB, halves_b, 1)
    gather_b = gather_plane(net, me, GB)
    next(gather_b)
    turn_over(GB, 1)
    next(gather_a)
    gz1.step(0)
    next(gather_b)
    next(gather_a)
    gz1.step(1)
    net.wait(heads, E.at[pl.ds(1, NZ - 1)])
    for d in range(NZ):
        A1[me.Z(-d), ROWS:PAD] = means(E[d, 0:1])
        A2[me.Z(-d), ROWS:PAD] = means(E[d, 1:2])
    next(gather_b)
    finish(gather_a)
    ones = jnp.ones((16, COLS), BF)

    def upstream(A, G, slot, dims, start):
        rows = pl.ds(16 * (slot % (G.shape[2] // 16)), 16)
        g = G[:, :, rows].reshape(COLS, COLS)
        squares = g * g
        if slot == 0:
            shape = (COLS, COLS)
            same = lax.broadcasted_iota(jnp.int32, shape, 0) == lax.broadcasted_iota(
                jnp.int32, shape, 1
            )
            squares = jnp.where(same, 0.0, squares.astype(F32)).astype(BF)
        u = dot(A[me.Z(SLOTS[slot])], g, ((1,), dims))
        s = dot(ones, squares, ((1,), dims))[0:8]
        if start:
            U[0:PAD] = u
            U[PAD : PAD + 8] = s
        else:
            U[0:PAD] += u
            U[PAD : PAD + 8] += s

    own_slope = diagonal.astype(BF).astype(F32) * sums[2:3]

    def down(v, A):
        level = U[ROWS : ROWS + 1] + U[ROWS + 1 : ROWS + 2]
        slope = U[PAD : PAD + 1] * (0.5 / offdiag_weight) + own_slope
        n = A[me.z, 0:ROWS].astype(F32)
        DN[view(v)] = ((U[0:ROWS] - level - n * slope) / spread[v]).astype(BF)

    def partial(v, T, V, d):
        b = me.Z(d)
        piece = W[pl.ds(2 * b, 2)].reshape(COLS, COLS)
        t = dot(DN[view(v)], piece, ((1,), (1,)))
        if d == 0:
            V[...] = t
        else:
            T[b] = t.astype(BF)

    for slot in range(4):
        upstream(A2, GA, slot, (0,), slot == 0)
    next(gather_b)
    gz1.step(2)
    net.wait(turned, turned_ref)
    gather_2 = gather_plane(net, me, G2)
    next(gather_2)
    finish(gather_b)
    for slot in range(4, 8):
        upstream(A2, GB, slot, (0,), False)
    down(0, A1)
    ring1 = ScatterZ(net, me, T1, R1)
    ring2 = ScatterZ(net, me, T2, R2)
    gz1.step(3)
    partial(0, T1, V1, 4)
    ring1.long(0)
    partial(0, T1, V1, 3)
    partial(0, T1, V1, -3)
    ring1.short(1)
    next(gather_2)
    partial(0, T1, V1, 2)
    partial(0, T1, V1, -2)
    ring1.long(1)
    ring1.short(2)
    partial(0, T1, V1, 1)
    partial(0, T1, V1, -1)
    next(gather_2)
    ring1.long(2)
    ring1.short(3)
    partial(0, T1, V1, 0)
    next(gather_2)
    ring1.long(3)
    finish(gather_2)
    for slot in range(8):
        upstream(A1, G2, slot, (1,), slot == 0)
    down(1, A2)
    partial(1, T2, V2, 4)
    ring2.long(0)
    partial(1, T2, V2, 3)
    partial(1, T2, V2, -3)
    ring2.short(1)
    partial(1, T2, V2, 2)
    partial(1, T2, V2, -2)
    weight = Blocks(net, me, PG, SG)

    def weight_block(b):
        weight.put(b, dot(H[:, pl.ds(b * COLS, COLS)], DN[...], ((0,), (0,))))

    for b in range(5):
        weight_block(b)
    ring2.long(1)
    for b in range(5, 8):
        weight_block(b)
    partial(1, T2, V2, 1)
    partial(1, T2, V2, -1)
    ring2.short(2)
    halves_g = []
    scatter_g = scatter_plane(net, me, SG, MG, FG, QG, LG, halves_g)
    weight.add()
    next(scatter_g)
    partial(1, T2, V2, 0)
    ring2.long(2)
    next(scatter_g)
    ring2.short(3)
    next(scatter_g)
    ring2.long(3)
    def writer(start):
        def write(row, value):
            out[start + row : start + row + 48] = value.astype(BF)

        return write

    ring1.finish(V1, writer(128))
    ring2.finish(V2, writer(128 + ROWS))
    finish(scatter_g)
    for o in (0, 1):
        out[64 * o : 64 * o + 64] = (halves_g[o] / math.sqrt(TOKENS)).astype(BF)
    net.drain()


def local(hidden_first, hidden_second, weight):
    vm = pl.BlockSpec(memory_space=pltpu.VMEM)
    hbm = pl.BlockSpec(memory_space=pl.ANY)
    senders, count = 27, 253
    out = pl.pallas_call(
        kernel,
        out_shape=jax.ShapeDtypeStruct((128 + 2 * ROWS, COLS), BF),
        in_specs=[hbm] * 3,
        out_specs=vm,
        scratch_shapes=[
            pltpu.VMEM((2 * ROWS, 4096), BF),
            pltpu.VMEM((16, 2, 128, COLS), BF),
            pltpu.VMEM((2 * ROWS, COLS), F32),
            pltpu.VMEM((2 * ROWS, COLS), BF),
            pltpu.VMEM((NZ, PAD, COLS), BF),
            pltpu.VMEM((NZ, PAD, COLS), BF),
            pltpu.VMEM((8, 4, COLS), F32),
            pltpu.VMEM((4, 4, COLS), F32),
            pltpu.VMEM((8, 4, COLS), F32),
            pltpu.VMEM((4, 4, COLS), F32),
            pltpu.VMEM((NZ, 2, COLS), F32),
            pltpu.VMEM((16, 2, 64, COLS), BF),
            pltpu.VMEM((16, 2, 64, COLS), BF),
            pltpu.VMEM((16, 2, 128, COLS), BF),
            pltpu.VMEM((PAD + 8, COLS), F32),
            pltpu.VMEM((NZ, ROWS, COLS), BF),
            pltpu.VMEM((2, 4, ROWS, COLS), BF),
            pltpu.VMEM((NZ, ROWS, COLS), BF),
            pltpu.VMEM((2, 4, ROWS, COLS), BF),
            pltpu.VMEM((ROWS, COLS), F32),
            pltpu.VMEM((ROWS, COLS), F32),
        ]
        + scatter_plane_scratch(64)
        + scatter_plane_scratch(64)
        + scatter_plane_scratch(128)
        + [
            pltpu.SemaphoreType.DMA((3,)),
            pltpu.SemaphoreType.DMA((senders,)),
            pltpu.SemaphoreType.DMA((count,)),
        ],
        compiler_params=pltpu.CompilerParams(
            collective_id=1, has_side_effects=True, vmem_limit_bytes=60 * 1024 * 1024
        ),
    )(hidden_first, hidden_second, weight)
    return out[:128], out[128 : 128 + ROWS], out[128 + ROWS :]


def solution(mesh):
    in_specs = (P("dp", None), P("dp", None), P("dp", "mp"))
    out_specs = (P("dp", "mp"), P("dp", "mp"), P("dp", "mp"))
    return jax.shard_map(local, mesh=mesh, in_specs=in_specs, out_specs=out_specs, check_vma=False)
```

```python
import math

import jax
import jax.numpy as jnp
from jax import lax
from jax.experimental import pallas as pl
from jax.experimental.pallas import tpu as pltpu
from jax.sharding import PartitionSpec as P

MESH = pl.DeviceIdType.MESH
BF = jnp.bfloat16
F32 = jnp.float32

epsilon = 1e-05
offdiag_weight = 0.0051

TOKENS = 6144
ROWS = 192
PAD = 208
COLS = 512
NZ = 8
SLOTS = (0, 1, -1, 2, -2, 3, -3, 4)


def wrap(value, size):
    return lax.rem(value + size, size)


class Place:
    def __init__(self):
        dp = lax.axis_index("dp")
        self.dp = dp
        self.x = lax.div(dp, 8)
        self.y = lax.rem(lax.div(dp, 2), 4)
        self.c = lax.rem(dp, 2)
        self.z = lax.axis_index("mp")

    def X(self, d):
        return wrap(self.x + d, 4)

    def Y(self, d):
        return wrap(self.y + d, 4)

    def Z(self, d):
        return wrap(self.z + d, NZ)

    def block(self, dx, dy, dc=0):
        return self.X(dx) * 8 + self.Y(dy) * 2 + wrap(self.c + dc, 2)

    def chip(self, dx, dy):
        return self.X(dx) * 4 + self.Y(dy)

    def at(self, dx, dy, dc=0):
        return {"dp": self.block(dx, dy, dc)}

    def sib(self):
        return {"dp": self.dp + 1 - 2 * self.c}

    def up(self, d):
        return {"mp": self.Z(d)}

    def plane_peers(self):
        row = [(0, dy, dc) for dy in range(4) for dc in range(2)][1:]
        column = [(dx, 0, 0) for dx in range(1, 4)]
        return [self.at(*p) for p in row + column]

    def z_peers(self):
        return [self.up(d) for d in range(1, NZ)]


class Net:
    def __init__(self, me, sent, recvs):
        self.me, self.sent, self.recvs = me, sent, recvs
        self.count = 0
        self.totals = []

    def group(self):
        self.count += 1
        return self.count - 1

    def sender(self, total):
        self.totals.append(total)
        return len(self.totals) - 1

    def copy(self, src, dst, to, sender, group):
        return pltpu.make_async_remote_copy(
            src_ref=src,
            dst_ref=dst,
            send_sem=self.sent.at[sender],
            recv_sem=self.recvs.at[group],
            device_id=to,
            device_id_type=MESH,
        )

    def send(self, src, dst, to, sender, group=None):
        copy = self.copy(src, dst, to, sender, self.group() if group is None else group)
        copy.start()
        return copy

    def wait(self, group, total):
        self.copy(total, total, self.me.sib(), 0, group).wait_recv()

    def drain(self):
        for sender, total in enumerate(self.totals):
            self.copy(total, total, self.me.sib(), sender, 0).wait_send()


def barrier(peers):
    sem = pltpu.get_barrier_semaphore()
    for peer in peers:
        pl.semaphore_signal(sem, inc=1, device_id=peer, device_id_type=MESH)
    pl.semaphore_wait(sem, len(peers))


def dot(a, b, dims):
    return lax.dot_general(a, b, ((dims[0], dims[1]), ((), ())), preferred_element_type=F32)


def turn(o, first, second):
    return (first, second) if o == 0 else (second, first)


def finish(steps):
    for _ in steps:
        pass


def advance(steps, count):
    for _ in range(count):
        next(steps)


def gather_plane(net, me, W):
    rows = W.shape[2]
    part, quarter = rows // 2, rows // 4

    def block(o, a, b):
        return me.chip(*turn(o, a, b))

    def to(o, a, b):
        return me.at(*turn(o, a, b))

    def push(index, start, size, target, group=None):
        ref = W.at[index, me.c, pl.ds(start, size)]
        return net.send(ref, ref, target, many, group)

    own = me.chip(0, 0)
    block_ref = W.at[own, me.c]
    both = [(o, d) for d in (1, -1) for o in (0, 1)]
    first, second = {}, {}
    shared, far = net.group(), [net.group() for _ in range(4)]
    many, one = net.sender(W.at[pl.ds(0, 15)]), net.sender(block_ref)

    def over(o, a):
        for d in (1, -1):
            second[o, a, d] = push(block(o, a, 0), part * o, part, to(o, 0, d))

    def share(o, a, b):
        push(block(o, a, b), part * o, part, me.sib(), shared)

    for d in (1, -1, 2):
        for o in (0, 1):
            first[o, d] = push(own, part * o, part, to(o, d, 0))
    for o in (0, 1):
        over(o, 0)
    net.send(block_ref, block_ref, me.sib(), one, shared)
    yield
    for d in (1, -1, 2):
        for o in (0, 1):
            first[o, d].wait_recv()
            over(o, -d)
        for o in (0, 1):
            share(o, -d, 0)
    yield
    for k, a in enumerate((0, -1, 1, -2)):
        for o, d in both:
            second[o, a, d].wait_recv()
            start = part * o + (0 if d == 1 else quarter)
            push(block(o, a, -d), start, quarter, to(o, 0, d), far[k])
        for o, d in both:
            share(o, a, -d)
        yield
    for k, a in enumerate((0, -1, 1, -2)):
        net.wait(far[k], block_ref)
        for o in (0, 1):
            share(o, a, 2)
    yield
    net.wait(shared, W.at[:, 1 - me.c])


def scatter_plane(net, me, S, M1, F1, Q, F2, result):
    half_rows = S.shape[2] // 2

    def index(o, d):
        return me.X(d) if o == 0 else me.Y(d)

    def other(o, d):
        return me.Y(d) if o == 0 else me.X(d)

    def part(o, d, start, size=2):
        rows = pl.ds(half_rows * o, half_rows)
        if o == 0:
            return (index(o, d), pl.ds(start, size), rows)
        return (pl.ds(start, size), index(o, d), rows)

    def to(o, a, b):
        return me.at(*turn(o, a, b))

    both = [(o, d) for d in (1, -1) for o in (0, 1)]
    slot = {1: 0, -1: 1, 2: 2}
    mid = {}
    many, few = net.sender(S.at[pl.ds(0, 3)]), net.sender(F2)
    parts = [net.group() for _ in (0, 1)]
    ends = [net.group() for _ in (0, 1)]
    for o, d in both:
        h = 0 if d == 1 else 2
        mid[o, d] = net.send(S.at[part(o, 2, h)], M1.at[o, slot[d]], to(o, d, 0), many)
    for o, d in both:
        h = 0 if d == 1 else 2
        there = F1.at[o, slot[d], pl.ds(2 - h, 2)]
        net.send(S.at[part(o, d, 2 - h)], there, to(o, d, 0), many, parts[o])
    yield
    for o, d in both:
        h = 0 if d == 1 else 2
        mid[o, d].wait_recv()
        S[part(o, d, h)] += M1[o, slot[d]]
        there = F1.at[o, slot[d], pl.ds(h, 2)]
        net.send(S.at[part(o, d, h)], there, to(o, d, 0), many, parts[o])
    yield
    for o in (0, 1):
        net.wait(parts[o], F1.at[o])
        total = S[part(o, 0, 0, 4)].astype(F32) + F1[o, 0].astype(F32) + F1[o, 1].astype(F32)
        Q[o] = total.astype(BF)
        for d in (1, -1, 2):
            net.send(Q.at[o, other(o, d)], F2.at[o, slot[d]], to(o, 0, d), few, ends[o])
    yield
    for o in (0, 1):
        net.wait(ends[o], F2.at[o])
        result.append(
            (Q[o, other(o, 0)].astype(F32) + F2[o, 0].astype(F32))
            + (F2[o, 1].astype(F32) + F2[o, 2].astype(F32))
        )


def scatter_plane_scratch(rows):
    return [
        pltpu.VMEM((4, 4, 2, rows, COLS), BF),
        pltpu.VMEM((4, 4, rows, COLS), BF),
        pltpu.VMEM((2, 2, 2, rows // 2, COLS), BF),
        pltpu.VMEM((2, 2, 4, rows // 2, COLS), BF),
        pltpu.VMEM((2, 4, rows // 2, COLS), BF),
        pltpu.VMEM((2, 3, rows // 2, COLS), BF),
    ]


class ScatterZ:
    def __init__(self, net, me, T, R):
        self.net, self.me, self.T, self.R = net, me, T, R
        self.sender = net.sender(T.at[pl.ds(0, NZ - 1)])
        self.copies = {}

    def send(self, d, s, piece):
        slot = 0 if d == 1 else 1
        index = self.me.Z(d * (4 - s))
        rows = pl.ds(48 * piece, 48)
        previous = self.copies.get((d, s - 1, piece))
        if previous is not None:
            previous.wait_recv()
            self.T[index, rows] += self.R[slot, s - 1, rows]
        self.copies[d, s, piece] = self.net.send(
            self.T.at[index, rows], self.R.at[slot, s, rows], self.me.up(d), self.sender
        )

    def long(self, s):
        for i in (0, 1):
            self.send(1, s, i)
            self.send(-1, s, 2 + i)

    def short(self, s):
        for i in (0, 1):
            self.send(1, s, 2 + i)
            self.send(-1, s, i)

    def finish(self, V, write):
        for piece in (2, 0, 3, 1):
            rows = pl.ds(48 * piece, 48)
            for d in (1, -1):
                self.copies[d, 3, piece].wait_recv()
            write(
                48 * piece,
                V[rows] + (self.R[0, 3, rows].astype(F32) + self.R[1, 3, rows].astype(F32)),
            )


def exchange(net, me, B1, B2, merge1, merge2):
    row, column = B1.at[pl.ds(1, 7)], B2.at[pl.ds(1, 3)]
    one, two = net.group(), net.group()
    by = net.sender(row), net.sender(column)
    for dy in range(4):
        for dc in range(2):
            if dy + dc > 0:
                net.send(B1.at[0], B1.at[2 * dy + dc], me.at(0, dy, dc), by[0], one)

    def middle():
        net.wait(one, row)
        B2[0] = merge1(B1)
        for dx in range(1, 4):
            net.send(B2.at[0], B2.at[dx], me.at(dx, 0, 0), by[1], two)

    def last():
        net.wait(two, column)
        return merge2(B2)

    return middle, last


def merge_moments(rows):
    def merge(B):
        count = B.shape[0]
        result = []
        for view in range(2):
            means = [B[k, 2 * view : 2 * view + 1] for k in range(count)]
            squares = [B[k, 2 * view + 1 : 2 * view + 2] for k in range(count)]
            mean = sum(means) / count
            square = sum(squares) + rows * sum((m - mean) * (m - mean) for m in means)
            result += [mean, square]
        return jnp.concatenate(result, axis=0)

    return merge


def merge_sums(B):
    return sum(B[k] for k in range(B.shape[0]))


class Pairs:
    def __init__(self, net, me, Pb, S):
        self.net, self.me, self.Pb, self.S = net, me, Pb, S
        self.group, self.sender = net.group(), net.sender(S)
        self.places = []

    def put(self, slot, value):
        rows = pl.ds(16 * slot, 16)
        self.Pb[:, :, :, rows] = value.astype(BF).reshape(4, 4, 2, 16, COLS)
        there = self.S.at[:, :, rows]
        other = self.Pb.at[:, :, 1 - self.me.c, rows]
        self.net.send(other, there, self.me.sib(), self.sender, self.group)
        self.places.append(slot)

    def add(self):
        self.net.wait(self.group, self.S)
        for slot in self.places:
            rows = pl.ds(16 * slot, 16)
            self.S[:, :, rows] += self.Pb[:, :, self.me.c, rows]


class Blocks:
    def __init__(self, net, me, Pb, S):
        self.net, self.me, self.Pb, self.S = net, me, Pb, S
        self.group, self.sender = net.group(), net.sender(S)
        self.places = []

    def where(self, b):
        return (b // 2, pl.ds(2 * (b % 2), 2))

    def put(self, b, value):
        where = self.where(b)
        self.Pb[where] = value.astype(BF).reshape(2, 2, 128, COLS)
        other = self.Pb.at[where + (1 - self.me.c,)]
        self.net.send(other, self.S.at[where], self.me.sib(), self.sender, self.group)
        self.places.append(where)

    def add(self):
        self.net.wait(self.group, self.S)
        for where in self.places:
            self.S[where] += self.Pb[where + (self.me.c,)]


class GatherZ:
    def __init__(self, net, me, A):
        self.net, self.me, self.A = net, me, A
        self.sender = net.sender(A.at[pl.ds(0, NZ - 1), pl.ds(0, ROWS)])
        self.copies = {}

    def order(self):
        return [(1, 0), (-1, 2), (1, 1), (-1, 3), (1, 2), (-1, 0), (1, 3), (-1, 1)]

    def send(self, s, d, piece):
        ref = self.A.at[self.me.Z(-d * s), pl.ds(48 * piece, 48)]
        self.copies[s, d, piece] = self.net.send(ref, ref, self.me.up(d), self.sender)

    def start(self):
        for d, piece in self.order():
            self.send(0, d, piece)

    def step(self, s, places=range(8)):
        for place, (d, piece) in enumerate(self.order()):
            if place in places and (s, d, piece) in self.copies:
                self.copies[s, d, piece].wait_recv()
                if s < 2 or (s == 2 and place < 4):
                    self.send(s + 1, d, piece)


def means(value):
    high = value.astype(BF)
    low = (value - high.astype(F32)).astype(BF)
    rest = jnp.zeros((PAD - ROWS - 2, COLS), BF)
    return jnp.concatenate([high, low, rest], axis=0)


def kernel(
    hf, hs, w, out,
    H, W, acc, DN, A1, A2, B1, B2, X1, X2, Y1, Y2, E, E2, GA, GB, G2, U, T1, R1, T2, R2, V1, V2, PF,
    PA, SA, MA, FA, QA, LA, PB, SB, MB, FB, QB, LB, PG, SG, MG, FG, QG, LG,
    lsem, ssem, rsem,
):
    me = Place()
    net = Net(me, ssem, rsem)
    own = me.block(0, 0)
    mine = (me.chip(0, 0), me.c)
    loads = [
        pltpu.make_async_copy(w, W.at[mine], lsem.at[0]),
        pltpu.make_async_copy(hf, H.at[pl.ds(0, ROWS)], lsem.at[1]),
        pltpu.make_async_copy(hs, H.at[pl.ds(ROWS, ROWS)], lsem.at[2]),
    ]
    for load in loads:
        load.start()
    barrier(me.plane_peers() + me.z_peers())
    loads[0].wait()
    finish(gather_plane(net, me, W))
    loads[1].wait()
    loads[2].wait()

    acc[...] = jnp.zeros_like(acc)

    def project(k, _):
        cols = pl.ds(pl.multiple_of(k * 1024, 1024), 1024)
        piece = W[pl.ds(4 * k, 4)].reshape(1024, COLS)
        acc[...] += jnp.dot(H[:, cols], piece, preferred_element_type=F32)
        return 0

    lax.fori_loop(0, 4, project, 0)

    def view(v):
        return slice(v * ROWS, (v + 1) * ROWS)

    local_mean = []
    for v, B in ((0, B1), (1, B2)):
        mean = jnp.sum(acc[view(v)], axis=0, keepdims=True) / ROWS
        shifted = acc[view(v)] - mean
        X1[0, 2 * v : 2 * v + 1] = mean
        X1[0, 2 * v + 1 : 2 * v + 2] = jnp.sum(shifted * shifted, axis=0, keepdims=True)
        B[me.z] = shifted.astype(BF)
        local_mean.append(mean)
    gz2 = GatherZ(net, me, B2)
    gz1 = GatherZ(net, me, B1)
    middle, last = exchange(net, me, X1, X2, merge_moments(ROWS), merge_moments(8 * ROWS))
    gz2.start()
    middle()
    gz2.step(0)
    moments = last()
    spread, moves = [], []
    for v in range(2):
        spread.append(jnp.sqrt(moments[2 * v + 1 : 2 * v + 2] / TOKENS + epsilon))
        moves.append((local_mean[v] - moments[2 * v : 2 * v + 1], 1.0 / spread[v]))
    E2[0] = jnp.concatenate(moves[1], axis=0)
    scales, scales_by = net.group(), net.sender(E2.at[pl.ds(1, NZ - 1)])
    for d in range(1, NZ):
        net.send(E2.at[0], E2.at[d], me.up(d), scales_by, scales)

    def normalize(A, B, offset, move, scale):
        b = me.Z(offset)
        A[b, 0:ROWS] = ((B[b].astype(F32) + move) * scale).astype(BF)

    def normalize2(slot):
        d = -SLOTS[slot] % NZ
        normalize(A2, B2, SLOTS[slot], E2[d, 0:1], E2[d, 1:2])

    normalize(A1, B1, 0, *moves[0])
    normalize(A2, B2, 0, *moves[1])
    n1, n2 = A1[me.z, 0:ROWS].astype(F32), A2[me.z, 0:ROWS].astype(F32)
    Y1[0, 0:1] = jnp.sum(n1, axis=0, keepdims=True)
    Y1[0, 1:2] = jnp.sum(n2, axis=0, keepdims=True)
    Y1[0, 2:3] = jnp.sum(n1 * n2, axis=0, keepdims=True)
    Y1[0, 3:4] = jnp.zeros((1, COLS), F32)
    middle, last = exchange(net, me, Y1, Y2, merge_sums, merge_sums)
    groups = (Pairs(net, me, PA, SA), Pairs(net, me, PB, SB))

    def correlate(slot):
        if slot > 0:
            normalize2(slot)
        value = dot(A2[me.Z(SLOTS[slot]), 0:ROWS], A1[me.z, 0:ROWS], ((0,), (0,)))
        groups[slot // 4].put(slot % 4, value)

    halves_a, halves_b = [], []
    scatter_a = scatter_plane(net, me, SA, MA, FA, QA, LA, halves_a)
    scatter_b = scatter_plane(net, me, SB, MB, FB, QB, LB, halves_b)
    gz2.step(1, range(4))
    correlate(0)
    gz2.step(1, range(4, 8))
    net.wait(scales, E2.at[pl.ds(1, NZ - 1)])
    correlate(1)
    correlate(2)
    middle()
    gz2.step(2, range(4))
    correlate(3)
    groups[0].add()
    next(scatter_a)
    correlate(4)
    sums = last() / TOKENS
    E[0, 0:2] = sums[0:2]
    E[0, 2:4] = jnp.concatenate(moves[0], axis=0)
    heads = net.group()
    heads_by = net.sender(E.at[pl.ds(1, NZ - 1)])
    for d in range(1, NZ):
        net.send(E.at[0], E.at[d], me.up(d), heads_by, heads)
    gz2.step(2, range(4, 8))
    correlate(5)
    correlate(6)
    next(scatter_a)
    gz2.step(3)
    gz1.start()
    correlate(7)
    groups[1].add()
    next(scatter_b)
    next(scatter_a)
    next(scatter_b)
    gz1.step(0)
    diagonal = 2.0 * (sums[2:3] - 1.0)

    def loss_grad(G, halves, group):
        for o in (0, 1):
            rows = pl.ds(32 * o, 32)
            value = (2.0 * offdiag_weight / TOKENS) * halves[o]
            if group == 0 and o == 0:
                row = lax.broadcasted_iota(jnp.int32, (32, COLS), 0)
                column = lax.broadcasted_iota(jnp.int32, (32, COLS), 1)
                same = jnp.logical_and(row < 16, row + 16 * own == column)
                value = jnp.where(same, diagonal, value)
            G[mine + (rows,)] = value.astype(BF)

    turned_ref = G2.at[mine + (pl.ds(0, 112),)]
    turned, turned_by = net.group(), net.sender(turned_ref)

    def turn_over(G, group):
        for k in range(4):
            slot = 4 * group + k
            offset = SLOTS[slot]
            source = G.at[mine + (pl.ds(16 * k, 16),)]
            if offset == 0:
                G2[mine + (pl.ds(0, 16),)] = G[mine + (pl.ds(0, 16),)]
            else:
                there = 7 if offset == 4 else SLOTS.index(-offset)
                target = G2.at[mine + (pl.ds(16 * there, 16),)]
                net.send(source, target, me.up(offset), turned_by, turned)

    finish(scatter_a)
    loss_grad(GA, halves_a, 0)
    gather_a = gather_plane(net, me, GA)
    next(gather_a)
    turn_over(GA, 0)
    next(scatter_b)
    next(gather_a)
    finish(scatter_b)
    loss_grad(GB, halves_b, 1)
    gather_b = gather_plane(net, me, GB)
    next(gather_b)
    turn_over(GB, 1)
    gz1.step(1)
    advance(gather_a, 4)
    next(gather_b)
    next(gather_a)
    net.wait(heads, E.at[pl.ds(1, NZ - 1)])
    for d in range(NZ):
        A1[me.Z(-d), ROWS:PAD] = means(E[d, 0:1])
        A2[me.Z(-d), ROWS:PAD] = means(E[d, 1:2])
    advance(gather_b, 4)
    net.wait(turned, turned_ref)
    gather_2 = gather_plane(net, me, G2)
    next(gather_2)
    gz1.step(2)
    finish(gather_a)
    ones = jnp.ones((16, COLS), BF)

    def upstream(A, G, slot, dims, start):
        rows = pl.ds(16 * (slot % (G.shape[2] // 16)), 16)
        g = G[:, :, rows].reshape(COLS, COLS)
        squares = g * g
        if slot == 0:
            shape = (COLS, COLS)
            same = lax.broadcasted_iota(jnp.int32, shape, 0) == lax.broadcasted_iota(
                jnp.int32, shape, 1
            )
            squares = jnp.where(same, 0.0, squares.astype(F32)).astype(BF)
        u = dot(A[me.Z(SLOTS[slot])], g, ((1,), dims))
        s = dot(ones, squares, ((1,), dims))[0:8]
        if start:
            U[0:PAD] = u
            U[PAD : PAD + 8] = s
        else:
            U[0:PAD] += u
            U[PAD : PAD + 8] += s

    own_slope = diagonal.astype(BF).astype(F32) * sums[2:3]

    def down(v, A):
        level = U[ROWS : ROWS + 1] + U[ROWS + 1 : ROWS + 2]
        slope = U[PAD : PAD + 1] * (0.5 / offdiag_weight) + own_slope
        n = A[me.z, 0:ROWS].astype(F32)
        DN[view(v)] = ((U[0:ROWS] - level - n * slope) / spread[v]).astype(BF)

    def partial(v, T, V, d):
        b = me.Z(d)
        piece = W[pl.ds(2 * b, 2)].reshape(COLS, COLS)
        t = dot(DN[view(v)], piece, ((1,), (1,)))
        if d == 0:
            V[...] = t
        else:
            T[b] = t.astype(BF)

    for slot in range(4):
        upstream(A2, GA, slot, (0,), slot == 0)
    next(gather_b)
    next(gather_2)
    finish(gather_b)
    for slot in range(4, 8):
        upstream(A2, GB, slot, (0,), False)
    down(0, A1)
    ring1 = ScatterZ(net, me, T1, R1)
    ring2 = ScatterZ(net, me, T2, R2)

    def weight_first(b):
        PF[b] = dot(H[0:ROWS, pl.ds(b * COLS, COLS)], DN[0:ROWS], ((0,), (0,)))

    partial(0, T1, V1, 4)
    ring1.long(0)
    partial(0, T1, V1, 3)
    partial(0, T1, V1, -3)
    ring1.short(1)
    next(gather_2)
    partial(0, T1, V1, 2)
    partial(0, T1, V1, -2)
    gz1.step(3)
    next(gather_2)
    weight_first(0)
    weight_first(1)
    ring1.long(1)
    next(gather_2)
    partial(0, T1, V1, 1)
    partial(0, T1, V1, -1)
    ring1.short(2)
    next(gather_2)
    weight_first(2)
    weight_first(3)
    partial(0, T1, V1, 0)
    ring1.long(2)
    weight_first(4)
    weight_first(5)
    next(gather_2)
    ring1.short(3)
    weight_first(6)
    weight_first(7)
    ring1.long(3)
    finish(gather_2)
    for slot in range(1, 8):
        d = -SLOTS[slot] % NZ
        normalize(A1, B1, SLOTS[slot], E[d, 2:3], E[d, 3:4])
    for slot in range(8):
        upstream(A1, G2, slot, (1,), slot == 0)
    down(1, A2)
    partial(1, T2, V2, 4)
    ring2.long(0)
    partial(1, T2, V2, 3)
    partial(1, T2, V2, -3)
    ring2.short(1)
    weight = Blocks(net, me, PG, SG)
    for b in range(8):
        second = dot(
            H[ROWS : 2 * ROWS, pl.ds(b * COLS, COLS)], DN[ROWS : 2 * ROWS], ((0,), (0,))
        )
        weight.put(b, PF[b] + second)
    partial(1, T2, V2, 2)
    partial(1, T2, V2, -2)
    ring2.long(1)
    halves_g = []
    scatter_g = scatter_plane(net, me, SG, MG, FG, QG, LG, halves_g)
    weight.add()
    next(scatter_g)
    partial(1, T2, V2, 1)
    partial(1, T2, V2, -1)
    ring2.short(2)
    partial(1, T2, V2, 0)
    ring2.long(2)
    next(scatter_g)
    ring2.short(3)
    ring2.long(3)
    def writer(start):
        def write(row, value):
            out[start + row : start + row + 48] = value.astype(BF)

        return write

    ring1.finish(V1, writer(128))
    next(scatter_g)
    ring2.finish(V2, writer(128 + ROWS))
    finish(scatter_g)
    for o in (0, 1):
        out[64 * o : 64 * o + 64] = (halves_g[o] / math.sqrt(TOKENS)).astype(BF)
    net.drain()


def local(hidden_first, hidden_second, weight):
    vm = pl.BlockSpec(memory_space=pltpu.VMEM)
    hbm = pl.BlockSpec(memory_space=pl.ANY)
    senders, count = 28, 254
    out = pl.pallas_call(
        kernel,
        out_shape=jax.ShapeDtypeStruct((128 + 2 * ROWS, COLS), BF),
        in_specs=[hbm] * 3,
        out_specs=vm,
        scratch_shapes=[
            pltpu.VMEM((2 * ROWS, 4096), BF),
            pltpu.VMEM((16, 2, 128, COLS), BF),
            pltpu.VMEM((2 * ROWS, COLS), F32),
            pltpu.VMEM((2 * ROWS, COLS), BF),
            pltpu.VMEM((NZ, PAD, COLS), BF),
            pltpu.VMEM((NZ, PAD, COLS), BF),
            pltpu.VMEM((NZ, ROWS, COLS), BF),
            pltpu.VMEM((NZ, ROWS, COLS), BF),
            pltpu.VMEM((8, 4, COLS), F32),
            pltpu.VMEM((4, 4, COLS), F32),
            pltpu.VMEM((8, 4, COLS), F32),
            pltpu.VMEM((4, 4, COLS), F32),
            pltpu.VMEM((NZ, 4, COLS), F32),
            pltpu.VMEM((NZ, 2, COLS), F32),
            pltpu.VMEM((16, 2, 64, COLS), BF),
            pltpu.VMEM((16, 2, 64, COLS), BF),
            pltpu.VMEM((16, 2, 128, COLS), BF),
            pltpu.VMEM((PAD + 8, COLS), F32),
            pltpu.VMEM((NZ, ROWS, COLS), BF),
            pltpu.VMEM((2, 4, ROWS, COLS), BF),
            pltpu.VMEM((NZ, ROWS, COLS), BF),
            pltpu.VMEM((2, 4, ROWS, COLS), BF),
            pltpu.VMEM((ROWS, COLS), F32),
            pltpu.VMEM((ROWS, COLS), F32),
            pltpu.VMEM((8, COLS, COLS), F32),
        ]
        + scatter_plane_scratch(64)
        + scatter_plane_scratch(64)
        + scatter_plane_scratch(128)
        + [
            pltpu.SemaphoreType.DMA((3,)),
            pltpu.SemaphoreType.DMA((senders,)),
            pltpu.SemaphoreType.DMA((count,)),
        ],
        compiler_params=pltpu.CompilerParams(
            collective_id=1, has_side_effects=True, vmem_limit_bytes=60 * 1024 * 1024
        ),
    )(hidden_first, hidden_second, weight)
    return out[:128], out[128 : 128 + ROWS], out[128 + ROWS :]


def solution(mesh):
    in_specs = (P("dp", None), P("dp", None), P("dp", "mp"))
    out_specs = (P("dp", "mp"), P("dp", "mp"), P("dp", "mp"))
    return jax.shard_map(local, mesh=mesh, in_specs=in_specs, out_specs=out_specs, check_vma=False)
```

```python
import math

import jax
import jax.numpy as jnp
from jax import lax
from jax.experimental import pallas as pl
from jax.experimental.pallas import tpu as pltpu
from jax.sharding import PartitionSpec as P

MESH = pl.DeviceIdType.MESH
BF = jnp.bfloat16
F32 = jnp.float32

epsilon = 1e-05
offdiag_weight = 0.0051

TOKENS = 6144
ROWS = 192
PAD = 208
COLS = 512
NZ = 8
SLOTS = (0, 1, -1, 2, -2, 3, -3, 4)


def wrap(value, size):
    return lax.rem(value + size, size)


class Place:
    def __init__(self):
        dp = lax.axis_index("dp")
        self.dp = dp
        self.x = lax.div(dp, 8)
        self.y = lax.rem(lax.div(dp, 2), 4)
        self.c = lax.rem(dp, 2)
        self.z = lax.axis_index("mp")

    def X(self, d):
        return wrap(self.x + d, 4)

    def Y(self, d):
        return wrap(self.y + d, 4)

    def Z(self, d):
        return wrap(self.z + d, NZ)

    def block(self, dx, dy, dc=0):
        return self.X(dx) * 8 + self.Y(dy) * 2 + wrap(self.c + dc, 2)

    def at(self, dx, dy, dc=0):
        return {"dp": self.block(dx, dy, dc)}

    def sib(self):
        return {"dp": self.dp + 1 - 2 * self.c}

    def up(self, d):
        return {"mp": self.Z(d)}

    def plane_peers(self):
        row = [(0, dy, dc) for dy in range(4) for dc in range(2)][1:]
        column = [(dx, 0, 0) for dx in range(1, 4)]
        return [self.at(*p) for p in row + column]

    def z_peers(self):
        return [self.up(d) for d in range(1, NZ)]


class Net:
    def __init__(self, me, sent, recvs):
        self.me, self.sent, self.recvs = me, sent, recvs
        self.count = 0
        self.totals = []

    def group(self):
        self.count += 1
        return self.count - 1

    def sender(self, total):
        self.totals.append(total)
        return len(self.totals) - 1

    def copy(self, src, dst, to, sender, group):
        return pltpu.make_async_remote_copy(
            src_ref=src,
            dst_ref=dst,
            send_sem=self.sent.at[sender],
            recv_sem=self.recvs.at[group],
            device_id=to,
            device_id_type=MESH,
        )

    def send(self, src, dst, to, sender, group=None):
        copy = self.copy(src, dst, to, sender, self.group() if group is None else group)
        copy.start()
        return copy

    def wait(self, group, total):
        self.copy(total, total, self.me.sib(), 0, group).wait_recv()

    def drain(self):
        for sender, total in enumerate(self.totals):
            self.copy(total, total, self.me.sib(), sender, 0).wait_send()


def barrier(peers):
    sem = pltpu.get_barrier_semaphore()
    for peer in peers:
        pl.semaphore_signal(sem, inc=1, device_id=peer, device_id_type=MESH)
    pl.semaphore_wait(sem, len(peers))


def dot(a, b, dims):
    return lax.dot_general(a, b, ((dims[0], dims[1]), ((), ())), preferred_element_type=F32)


def turn(o, first, second):
    return (first, second) if o == 0 else (second, first)


def finish(steps):
    for _ in steps:
        pass


def advance(steps, count):
    for _ in range(count):
        next(steps)


def gather_plane(net, me, W):
    rows = W.shape[3]
    part, quarter = rows // 2, rows // 4

    def block(o, a, b):
        da, db = turn(o, a, b)
        return me.X(da), me.Y(db)

    def to(o, a, b):
        return me.at(*turn(o, a, b))

    def push(index, start, size, target, sender, group=None):
        ref = W.at[index + (me.c, pl.ds(start, size))]
        return net.send(ref, ref, target, sender, group)

    own = (me.X(0), me.Y(0))
    block_ref = W.at[own + (me.c,)]
    both = [(o, d) for d in (1, -1) for o in (0, 1)]
    first, second = {}, {}
    shared, far = net.group(), [net.group() for _ in range(4)]
    by_first, by_second = net.sender(W.at[0, pl.ds(0, 3), 0]), net.sender(W.at[0])
    by_far, by_shared = net.sender(W.at[0, pl.ds(0, 2)]), net.sender(W.at[:, :, 0])

    def over(o, a):
        for d in (1, -1):
            second[o, a, d] = push(block(o, a, 0), part * o, part, to(o, 0, d), by_second)

    def share(o, a):
        line = (me.X(a), slice(None)) if o == 0 else (slice(None), me.Y(a))
        ref = W.at[line + (me.c, pl.ds(part * o, part))]
        net.send(ref, ref, me.sib(), by_shared, shared)

    for d in (1, -1, 2):
        for o in (0, 1):
            first[o, d] = push(own, part * o, part, to(o, d, 0), by_first)
    for o in (0, 1):
        over(o, 0)
    yield
    for d in (1, -1, 2):
        for o in (0, 1):
            first[o, d].wait_recv()
            over(o, -d)
    yield
    for k, a in enumerate((0, -1, 1, -2)):
        for o, d in both:
            second[o, a, d].wait_recv()
            start = part * o + (0 if d == 1 else quarter)
            push(block(o, a, -d), start, quarter, to(o, 0, d), by_far, far[k])
        yield
    for k, a in enumerate((0, -1, 1, -2)):
        net.wait(far[k], block_ref)
        for o in (0, 1):
            share(o, a)
    yield
    net.wait(shared, W.at[:, :, 1 - me.c])


def scatter_plane(net, me, S, M1, F1, Q, F2, result):
    half_rows = S.shape[2] // 2

    def index(o, d):
        return me.X(d) if o == 0 else me.Y(d)

    def other(o, d):
        return me.Y(d) if o == 0 else me.X(d)

    def part(o, d, start, size=2):
        rows = pl.ds(half_rows * o, half_rows)
        if o == 0:
            return (index(o, d), pl.ds(start, size), rows)
        return (pl.ds(start, size), index(o, d), rows)

    def to(o, a, b):
        return me.at(*turn(o, a, b))

    both = [(o, d) for d in (1, -1) for o in (0, 1)]
    slot = {1: 0, -1: 1, 2: 2}
    mid = {}
    many, few = net.sender(S.at[pl.ds(0, 3)]), net.sender(F2)
    parts = [net.group() for _ in (0, 1)]
    ends = [net.group() for _ in (0, 1)]
    for o, d in both:
        h = 0 if d == 1 else 2
        mid[o, d] = net.send(S.at[part(o, 2, h)], M1.at[o, slot[d]], to(o, d, 0), many)
    for o, d in both:
        h = 0 if d == 1 else 2
        there = F1.at[o, slot[d], pl.ds(2 - h, 2)]
        net.send(S.at[part(o, d, 2 - h)], there, to(o, d, 0), many, parts[o])
    yield
    for o, d in both:
        h = 0 if d == 1 else 2
        mid[o, d].wait_recv()
        S[part(o, d, h)] += M1[o, slot[d]]
        there = F1.at[o, slot[d], pl.ds(h, 2)]
        net.send(S.at[part(o, d, h)], there, to(o, d, 0), many, parts[o])
    yield
    for o in (0, 1):
        net.wait(parts[o], F1.at[o])
        total = S[part(o, 0, 0, 4)].astype(F32) + F1[o, 0].astype(F32) + F1[o, 1].astype(F32)
        Q[o] = total.astype(BF)
        for d in (1, -1, 2):
            net.send(Q.at[o, other(o, d)], F2.at[o, slot[d]], to(o, 0, d), few, ends[o])
    yield
    for o in (0, 1):
        net.wait(ends[o], F2.at[o])
        result.append(
            (Q[o, other(o, 0)].astype(F32) + F2[o, 0].astype(F32))
            + (F2[o, 1].astype(F32) + F2[o, 2].astype(F32))
        )


def scatter_plane_scratch(rows):
    return [
        pltpu.VMEM((4, 4, 2, rows, COLS), BF),
        pltpu.VMEM((4, 4, rows, COLS), BF),
        pltpu.VMEM((2, 2, 2, rows // 2, COLS), BF),
        pltpu.VMEM((2, 2, 4, rows // 2, COLS), BF),
        pltpu.VMEM((2, 4, rows // 2, COLS), BF),
        pltpu.VMEM((2, 3, rows // 2, COLS), BF),
    ]


class ScatterZ:
    def __init__(self, net, me, T, R):
        self.net, self.me, self.T, self.R = net, me, T, R
        self.sender = net.sender(T.at[pl.ds(0, NZ - 1)])
        self.copies = {}

    def send(self, d, s, piece):
        slot = 0 if d == 1 else 1
        index = self.me.Z(d * (4 - s))
        rows = pl.ds(48 * piece, 48)
        previous = self.copies.get((d, s - 1, piece))
        if previous is not None:
            previous.wait_recv()
            self.T[index, rows] += self.R[slot, s - 1, rows]
        self.copies[d, s, piece] = self.net.send(
            self.T.at[index, rows], self.R.at[slot, s, rows], self.me.up(d), self.sender
        )

    def long(self, s):
        for i in (0, 1):
            self.send(1, s, i)
            self.send(-1, s, 2 + i)

    def short(self, s):
        for i in (0, 1):
            self.send(1, s, 2 + i)
            self.send(-1, s, i)

    def finish(self, V, write):
        for piece in (2, 0, 3, 1):
            rows = pl.ds(48 * piece, 48)
            for d in (1, -1):
                self.copies[d, 3, piece].wait_recv()
            write(
                48 * piece,
                V[rows] + (self.R[0, 3, rows].astype(F32) + self.R[1, 3, rows].astype(F32)),
            )


def exchange(net, me, B1, B2, merge1, merge2):
    row, column = B1.at[pl.ds(1, 7)], B2.at[pl.ds(1, 3)]
    one, two = net.group(), net.group()
    by = net.sender(row), net.sender(column)
    for dy in range(4):
        for dc in range(2):
            if dy + dc > 0:
                net.send(B1.at[0], B1.at[2 * dy + dc], me.at(0, dy, dc), by[0], one)

    def middle():
        net.wait(one, row)
        B2[0] = merge1(B1)
        for dx in range(1, 4):
            net.send(B2.at[0], B2.at[dx], me.at(dx, 0, 0), by[1], two)

    def last():
        net.wait(two, column)
        return merge2(B2)

    return middle, last


def merge_moments(rows):
    def merge(B):
        count = B.shape[0]
        result = []
        for view in range(2):
            means = [B[k, 2 * view : 2 * view + 1] for k in range(count)]
            squares = [B[k, 2 * view + 1 : 2 * view + 2] for k in range(count)]
            mean = sum(means) / count
            square = sum(squares) + rows * sum((m - mean) * (m - mean) for m in means)
            result += [mean, square]
        return jnp.concatenate(result, axis=0)

    return merge


def merge_sums(B):
    return sum(B[k] for k in range(B.shape[0]))


class Pairs:
    def __init__(self, net, me, Pb, S):
        self.net, self.me, self.Pb, self.S = net, me, Pb, S
        self.group, self.sender = net.group(), net.sender(S)
        self.places = []

    def put(self, slot, value):
        rows = pl.ds(16 * slot, 16)
        self.Pb[:, :, :, rows] = value.astype(BF).reshape(4, 4, 2, 16, COLS)
        there = self.S.at[:, :, rows]
        other = self.Pb.at[:, :, 1 - self.me.c, rows]
        self.net.send(other, there, self.me.sib(), self.sender, self.group)
        self.places.append(slot)

    def add(self):
        self.net.wait(self.group, self.S)
        for slot in self.places:
            rows = pl.ds(16 * slot, 16)
            self.S[:, :, rows] += self.Pb[:, :, self.me.c, rows]


class Blocks:
    def __init__(self, net, me, Pb, S):
        self.net, self.me, self.Pb, self.S = net, me, Pb, S
        self.group, self.sender = net.group(), net.sender(S)
        self.places = []

    def where(self, b):
        return (b // 2, pl.ds(2 * (b % 2), 2))

    def put(self, b, value):
        where = self.where(b)
        self.Pb[where] = value.astype(BF).reshape(2, 2, 128, COLS)
        other = self.Pb.at[where + (1 - self.me.c,)]
        self.net.send(other, self.S.at[where], self.me.sib(), self.sender, self.group)
        self.places.append(where)

    def add(self):
        self.net.wait(self.group, self.S)
        for where in self.places:
            self.S[where] += self.Pb[where + (self.me.c,)]


class GatherZ:
    def __init__(self, net, me, A):
        self.net, self.me, self.A = net, me, A
        self.sender = net.sender(A.at[pl.ds(0, NZ - 1), pl.ds(0, ROWS)])
        self.copies = {}

    def order(self):
        return [(1, 0), (-1, 2), (1, 1), (-1, 3), (1, 2), (-1, 0), (1, 3), (-1, 1)]

    def send(self, s, d, piece):
        ref = self.A.at[self.me.Z(-d * s), pl.ds(48 * piece, 48)]
        self.copies[s, d, piece] = self.net.send(ref, ref, self.me.up(d), self.sender)

    def start(self):
        for d, piece in self.order():
            self.send(0, d, piece)

    def step(self, s, places=range(8)):
        for place, (d, piece) in enumerate(self.order()):
            if place in places and (s, d, piece) in self.copies:
                self.copies[s, d, piece].wait_recv()
                if s < 2 or (s == 2 and place < 4):
                    self.send(s + 1, d, piece)


def means(value):
    high = value.astype(BF)
    low = (value - high.astype(F32)).astype(BF)
    rest = jnp.zeros((PAD - ROWS - 2, COLS), BF)
    return jnp.concatenate([high, low, rest], axis=0)


def kernel(
    hf, hs, w, out,
    H, W, acc, DN, A1, A2, B1, B2, X1, X2, Y1, Y2, E, E2, GA, GB, G2, U, T1, R1, T2, R2, V1, V2, PF,
    PA, SA, MA, FA, QA, LA, PB, SB, MB, FB, QB, LB, PG, SG, MG, FG, QG, LG,
    lsem, ssem, rsem,
):
    me = Place()
    net = Net(me, ssem, rsem)
    own = me.block(0, 0)
    mine = (me.x, me.y, me.c)
    loads = [
        pltpu.make_async_copy(w, W.at[mine], lsem.at[0]),
        pltpu.make_async_copy(hf, H.at[pl.ds(0, ROWS)], lsem.at[1]),
        pltpu.make_async_copy(hs, H.at[pl.ds(ROWS, ROWS)], lsem.at[2]),
    ]
    for load in loads:
        load.start()
    barrier(me.plane_peers() + me.z_peers())
    loads[0].wait()
    finish(gather_plane(net, me, W))
    loads[1].wait()
    loads[2].wait()

    acc[...] = jnp.zeros_like(acc)

    def project(k, _):
        cols = pl.ds(pl.multiple_of(k * 1024, 1024), 1024)
        piece = W[k].reshape(1024, COLS)
        acc[...] += jnp.dot(H[:, cols], piece, preferred_element_type=F32)
        return 0

    lax.fori_loop(0, 4, project, 0)

    def view(v):
        return slice(v * ROWS, (v + 1) * ROWS)

    local_mean = []
    for v, B in ((0, B1), (1, B2)):
        mean = jnp.sum(acc[view(v)], axis=0, keepdims=True) / ROWS
        shifted = acc[view(v)] - mean
        X1[0, 2 * v : 2 * v + 1] = mean
        X1[0, 2 * v + 1 : 2 * v + 2] = jnp.sum(shifted * shifted, axis=0, keepdims=True)
        B[me.z] = shifted.astype(BF)
        local_mean.append(mean)
    gz2 = GatherZ(net, me, B2)
    gz1 = GatherZ(net, me, B1)
    middle, last = exchange(net, me, X1, X2, merge_moments(ROWS), merge_moments(8 * ROWS))
    gz2.start()
    middle()
    gz2.step(0)
    moments = last()
    spread, moves = [], []
    for v in range(2):
        spread.append(jnp.sqrt(moments[2 * v + 1 : 2 * v + 2] / TOKENS + epsilon))
        moves.append((local_mean[v] - moments[2 * v : 2 * v + 1], 1.0 / spread[v]))
    E2[0] = jnp.concatenate(moves[1], axis=0)
    scales, scales_by = net.group(), net.sender(E2.at[pl.ds(1, NZ - 1)])
    for d in range(1, NZ):
        net.send(E2.at[0], E2.at[d], me.up(d), scales_by, scales)

    def normalize(A, B, offset, move, scale):
        b = me.Z(offset)
        A[b, 0:ROWS] = ((B[b].astype(F32) + move) * scale).astype(BF)

    def normalize2(slot):
        d = -SLOTS[slot] % NZ
        normalize(A2, B2, SLOTS[slot], E2[d, 0:1], E2[d, 1:2])

    normalize(A1, B1, 0, *moves[0])
    normalize(A2, B2, 0, *moves[1])
    n1, n2 = A1[me.z, 0:ROWS].astype(F32), A2[me.z, 0:ROWS].astype(F32)
    Y1[0, 0:1] = jnp.sum(n1, axis=0, keepdims=True)
    Y1[0, 1:2] = jnp.sum(n2, axis=0, keepdims=True)
    Y1[0, 2:3] = jnp.sum(n1 * n2, axis=0, keepdims=True)
    Y1[0, 3:4] = jnp.zeros((1, COLS), F32)
    middle, last = exchange(net, me, Y1, Y2, merge_sums, merge_sums)
    groups = (Pairs(net, me, PA, SA), Pairs(net, me, PB, SB))

    def correlate(slot):
        if slot > 0:
            normalize2(slot)
        value = dot(A2[me.Z(SLOTS[slot]), 0:ROWS], A1[me.z, 0:ROWS], ((0,), (0,)))
        groups[slot // 4].put(slot % 4, value)

    halves_a, halves_b = [], []
    scatter_a = scatter_plane(net, me, SA, MA, FA, QA, LA, halves_a)
    scatter_b = scatter_plane(net, me, SB, MB, FB, QB, LB, halves_b)
    gz2.step(1, range(4))
    correlate(0)
    gz2.step(1, range(4, 8))
    net.wait(scales, E2.at[pl.ds(1, NZ - 1)])
    correlate(1)
    correlate(2)
    middle()
    gz2.step(2, range(4))
    correlate(3)
    groups[0].add()
    next(scatter_a)
    correlate(4)
    sums = last() / TOKENS
    E[0, 0:2] = sums[0:2]
    E[0, 2:4] = jnp.concatenate(moves[0], axis=0)
    heads = net.group()
    heads_by = net.sender(E.at[pl.ds(1, NZ - 1)])
    for d in range(1, NZ):
        net.send(E.at[0], E.at[d], me.up(d), heads_by, heads)
    gz2.step(2, range(4, 8))
    correlate(5)
    correlate(6)
    next(scatter_a)
    gz2.step(3)
    gz1.start()
    correlate(7)
    groups[1].add()
    next(scatter_b)
    next(scatter_a)
    next(scatter_b)
    gz1.step(0)
    diagonal = 2.0 * (sums[2:3] - 1.0)

    def loss_grad(G, halves, group):
        for o in (0, 1):
            rows = pl.ds(32 * o, 32)
            value = (2.0 * offdiag_weight / TOKENS) * halves[o]
            if group == 0 and o == 0:
                row = lax.broadcasted_iota(jnp.int32, (32, COLS), 0)
                column = lax.broadcasted_iota(jnp.int32, (32, COLS), 1)
                same = jnp.logical_and(row < 16, row + 16 * own == column)
                value = jnp.where(same, diagonal, value)
            G[mine + (rows,)] = value.astype(BF)

    turned_ref = G2.at[mine + (pl.ds(0, 112),)]
    turned, turned_by = net.group(), net.sender(turned_ref)

    def turn_over(G, group):
        for k in range(4):
            slot = 4 * group + k
            offset = SLOTS[slot]
            source = G.at[mine + (pl.ds(16 * k, 16),)]
            if offset == 0:
                G2[mine + (pl.ds(0, 16),)] = G[mine + (pl.ds(0, 16),)]
            else:
                there = 7 if offset == 4 else SLOTS.index(-offset)
                target = G2.at[mine + (pl.ds(16 * there, 16),)]
                net.send(source, target, me.up(offset), turned_by, turned)

    finish(scatter_a)
    loss_grad(GA, halves_a, 0)
    gather_a = gather_plane(net, me, GA)
    next(gather_a)
    turn_over(GA, 0)
    next(scatter_b)
    next(gather_a)
    finish(scatter_b)
    loss_grad(GB, halves_b, 1)
    gather_b = gather_plane(net, me, GB)
    next(gather_b)
    turn_over(GB, 1)
    gz1.step(1)
    advance(gather_a, 4)
    next(gather_b)
    next(gather_a)
    net.wait(heads, E.at[pl.ds(1, NZ - 1)])
    for d in range(NZ):
        A1[me.Z(-d), ROWS:PAD] = means(E[d, 0:1])
        A2[me.Z(-d), ROWS:PAD] = means(E[d, 1:2])
    advance(gather_b, 4)
    net.wait(turned, turned_ref)
    gather_2 = gather_plane(net, me, G2)
    next(gather_2)
    gz1.step(2)
    finish(gather_a)
    ones = jnp.ones((16, COLS), BF)

    def upstream(A, G, slot, dims, start):
        rows = pl.ds(16 * (slot % (G.shape[3] // 16)), 16)
        g = G[:, :, :, rows].reshape(COLS, COLS)
        squares = g * g
        if slot == 0:
            shape = (COLS, COLS)
            same = lax.broadcasted_iota(jnp.int32, shape, 0) == lax.broadcasted_iota(
                jnp.int32, shape, 1
            )
            squares = jnp.where(same, 0.0, squares.astype(F32)).astype(BF)
        u = dot(A[me.Z(SLOTS[slot])], g, ((1,), dims))
        s = dot(ones, squares, ((1,), dims))[0:8]
        if start:
            U[0:PAD] = u
            U[PAD : PAD + 8] = s
        else:
            U[0:PAD] += u
            U[PAD : PAD + 8] += s

    own_slope = diagonal.astype(BF).astype(F32) * sums[2:3]

    def down(v, A):
        level = U[ROWS : ROWS + 1] + U[ROWS + 1 : ROWS + 2]
        slope = U[PAD : PAD + 1] * (0.5 / offdiag_weight) + own_slope
        n = A[me.z, 0:ROWS].astype(F32)
        DN[view(v)] = ((U[0:ROWS] - level - n * slope) / spread[v]).astype(BF)

    def partial(v, T, V, d):
        b = me.Z(d)
        piece = W[lax.div(b, 2), pl.ds(2 * lax.rem(b, 2), 2)].reshape(COLS, COLS)
        t = dot(DN[view(v)], piece, ((1,), (1,)))
        if d == 0:
            V[...] = t
        else:
            T[b] = t.astype(BF)

    for slot in range(4):
        upstream(A2, GA, slot, (0,), slot == 0)
    next(gather_b)
    next(gather_2)
    finish(gather_b)
    for slot in range(4, 8):
        upstream(A2, GB, slot, (0,), False)
    down(0, A1)
    ring1 = ScatterZ(net, me, T1, R1)
    ring2 = ScatterZ(net, me, T2, R2)

    def weight_first(b):
        PF[b] = dot(H[0:ROWS, pl.ds(b * COLS, COLS)], DN[0:ROWS], ((0,), (0,)))

    partial(0, T1, V1, 4)
    ring1.long(0)
    partial(0, T1, V1, 3)
    partial(0, T1, V1, -3)
    ring1.short(1)
    next(gather_2)
    partial(0, T1, V1, 2)
    partial(0, T1, V1, -2)
    gz1.step(3)
    next(gather_2)
    weight_first(0)
    weight_first(1)
    ring1.long(1)
    next(gather_2)
    partial(0, T1, V1, 1)
    partial(0, T1, V1, -1)
    ring1.short(2)
    next(gather_2)
    weight_first(2)
    weight_first(3)
    partial(0, T1, V1, 0)
    ring1.long(2)
    weight_first(4)
    weight_first(5)
    for slot in range(1, 8):
        d = -SLOTS[slot] % NZ
        normalize(A1, B1, SLOTS[slot], E[d, 2:3], E[d, 3:4])
    next(gather_2)
    ring1.short(3)
    weight_first(6)
    weight_first(7)
    ring1.long(3)
    finish(gather_2)
    for slot in range(8):
        upstream(A1, G2, slot, (1,), slot == 0)
    down(1, A2)
    partial(1, T2, V2, 4)
    ring2.long(0)
    partial(1, T2, V2, 3)
    partial(1, T2, V2, -3)
    ring2.short(1)
    weight = Blocks(net, me, PG, SG)
    for b in range(8):
        second = dot(
            H[ROWS : 2 * ROWS, pl.ds(b * COLS, COLS)], DN[ROWS : 2 * ROWS], ((0,), (0,))
        )
        weight.put(b, PF[b] + second)
    partial(1, T2, V2, 2)
    partial(1, T2, V2, -2)
    ring2.long(1)
    halves_g = []
    scatter_g = scatter_plane(net, me, SG, MG, FG, QG, LG, halves_g)
    weight.add()
    next(scatter_g)
    partial(1, T2, V2, 1)
    partial(1, T2, V2, -1)
    ring2.short(2)
    partial(1, T2, V2, 0)
    ring2.long(2)
    next(scatter_g)
    ring2.short(3)
    ring2.long(3)
    def writer(start):
        def write(row, value):
            out[start + row : start + row + 48] = value.astype(BF)

        return write

    ring1.finish(V1, writer(128))
    next(scatter_g)
    ring2.finish(V2, writer(128 + ROWS))
    finish(scatter_g)
    for o in (0, 1):
        out[64 * o : 64 * o + 64] = (halves_g[o] / math.sqrt(TOKENS)).astype(BF)
    net.drain()


def local(hidden_first, hidden_second, weight):
    vm = pl.BlockSpec(memory_space=pltpu.VMEM)
    hbm = pl.BlockSpec(memory_space=pl.ANY)
    senders, count = 36, 254
    out = pl.pallas_call(
        kernel,
        out_shape=jax.ShapeDtypeStruct((128 + 2 * ROWS, COLS), BF),
        in_specs=[hbm] * 3,
        out_specs=vm,
        scratch_shapes=[
            pltpu.VMEM((2 * ROWS, 4096), BF),
            pltpu.VMEM((4, 4, 2, 128, COLS), BF),
            pltpu.VMEM((2 * ROWS, COLS), F32),
            pltpu.VMEM((2 * ROWS, COLS), BF),
            pltpu.VMEM((NZ, PAD, COLS), BF),
            pltpu.VMEM((NZ, PAD, COLS), BF),
            pltpu.VMEM((NZ, ROWS, COLS), BF),
            pltpu.VMEM((NZ, ROWS, COLS), BF),
            pltpu.VMEM((8, 4, COLS), F32),
            pltpu.VMEM((4, 4, COLS), F32),
            pltpu.VMEM((8, 4, COLS), F32),
            pltpu.VMEM((4, 4, COLS), F32),
            pltpu.VMEM((NZ, 4, COLS), F32),
            pltpu.VMEM((NZ, 2, COLS), F32),
            pltpu.VMEM((4, 4, 2, 64, COLS), BF),
            pltpu.VMEM((4, 4, 2, 64, COLS), BF),
            pltpu.VMEM((4, 4, 2, 128, COLS), BF),
            pltpu.VMEM((PAD + 8, COLS), F32),
            pltpu.VMEM((NZ, ROWS, COLS), BF),
            pltpu.VMEM((2, 4, ROWS, COLS), BF),
            pltpu.VMEM((NZ, ROWS, COLS), BF),
            pltpu.VMEM((2, 4, ROWS, COLS), BF),
            pltpu.VMEM((ROWS, COLS), F32),
            pltpu.VMEM((ROWS, COLS), F32),
            pltpu.VMEM((8, COLS, COLS), F32),
        ]
        + scatter_plane_scratch(64)
        + scatter_plane_scratch(64)
        + scatter_plane_scratch(128)
        + [
            pltpu.SemaphoreType.DMA((3,)),
            pltpu.SemaphoreType.DMA((senders,)),
            pltpu.SemaphoreType.DMA((count,)),
        ],
        compiler_params=pltpu.CompilerParams(
            collective_id=1, has_side_effects=True, vmem_limit_bytes=60 * 1024 * 1024
        ),
    )(hidden_first, hidden_second, weight)
    return out[:128], out[128 : 128 + ROWS], out[128 + ROWS :]


def solution(mesh):
    in_specs = (P("dp", None), P("dp", None), P("dp", "mp"))
    out_specs = (P("dp", "mp"), P("dp", "mp"), P("dp", "mp"))
    return jax.shard_map(local, mesh=mesh, in_specs=in_specs, out_specs=out_specs, check_vma=False)
```

```python
import math

import jax
import jax.numpy as jnp
from jax import lax
from jax.experimental import pallas as pl
from jax.experimental.pallas import tpu as pltpu
from jax.sharding import PartitionSpec as P

MESH = pl.DeviceIdType.MESH
BF = jnp.bfloat16
F32 = jnp.float32

epsilon = 1e-05
offdiag_weight = 0.0051

TOKENS = 6144
ROWS = 192
PAD = 208
COLS = 512
NZ = 8
SLOTS = (0, 1, -1, 2, -2, 3, -3, 4)


def wrap(value, size):
    return lax.rem(value + size, size)


class Place:
    def __init__(self):
        dp = lax.axis_index("dp")
        self.dp = dp
        self.x = lax.div(dp, 8)
        self.y = lax.rem(lax.div(dp, 2), 4)
        self.c = lax.rem(dp, 2)
        self.z = lax.axis_index("mp")

    def X(self, d):
        return wrap(self.x + d, 4)

    def Y(self, d):
        return wrap(self.y + d, 4)

    def Z(self, d):
        return wrap(self.z + d, NZ)

    def block(self, dx, dy, dc=0):
        return self.X(dx) * 8 + self.Y(dy) * 2 + wrap(self.c + dc, 2)

    def at(self, dx, dy, dc=0):
        return {"dp": self.block(dx, dy, dc)}

    def sib(self):
        return {"dp": self.dp + 1 - 2 * self.c}

    def up(self, d):
        return {"mp": self.Z(d)}

    def plane_peers(self):
        row = [(0, dy, dc) for dy in range(4) for dc in range(2)][1:]
        column = [(dx, 0, 0) for dx in range(1, 4)]
        return [self.at(*p) for p in row + column]

    def z_peers(self):
        return [self.up(d) for d in range(1, NZ)]


class Net:
    def __init__(self, me, sent, recvs):
        self.me, self.sent, self.recvs = me, sent, recvs
        self.count = 0
        self.totals = []

    def group(self):
        self.count += 1
        return self.count - 1

    def sender(self, total):
        self.totals.append(total)
        return len(self.totals) - 1

    def copy(self, src, dst, to, sender, group):
        return pltpu.make_async_remote_copy(
            src_ref=src,
            dst_ref=dst,
            send_sem=self.sent.at[sender],
            recv_sem=self.recvs.at[group],
            device_id=to,
            device_id_type=MESH,
        )

    def send(self, src, dst, to, sender, group=None):
        copy = self.copy(src, dst, to, sender, self.group() if group is None else group)
        copy.start()
        return copy

    def wait(self, group, total):
        self.copy(total, total, self.me.sib(), 0, group).wait_recv()

    def drain(self):
        for sender, total in enumerate(self.totals):
            self.copy(total, total, self.me.sib(), sender, 0).wait_send()


def barrier(peers):
    sem = pltpu.get_barrier_semaphore()
    for peer in peers:
        pl.semaphore_signal(sem, inc=1, device_id=peer, device_id_type=MESH)
    pl.semaphore_wait(sem, len(peers))


def dot(a, b, dims):
    return lax.dot_general(a, b, ((dims[0], dims[1]), ((), ())), preferred_element_type=F32)


def turn(o, first, second):
    return (first, second) if o == 0 else (second, first)


def finish(steps):
    for _ in steps:
        pass


def advance(steps, count):
    for _ in range(count):
        next(steps)


def gather_plane(net, me, W):
    rows = W.shape[3]
    part, quarter = rows // 2, rows // 4

    def block(o, a, b):
        da, db = turn(o, a, b)
        return me.X(da), me.Y(db)

    def to(o, a, b):
        return me.at(*turn(o, a, b))

    def push(index, start, size, target, sender, group=None):
        ref = W.at[index + (me.c, pl.ds(start, size))]
        return net.send(ref, ref, target, sender, group)

    own = (me.X(0), me.Y(0))
    block_ref = W.at[own + (me.c,)]
    both = [(o, d) for d in (1, -1) for o in (0, 1)]
    first, second = {}, {}
    shared, far = net.group(), [net.group() for _ in range(4)]
    by_first, by_second = net.sender(W.at[0, pl.ds(0, 3), 0]), net.sender(W.at[0])
    by_far, by_shared = net.sender(W.at[0, pl.ds(0, 2)]), net.sender(W.at[:, :, 0])

    def over(o, a):
        for d in (1, -1):
            second[o, a, d] = push(block(o, a, 0), part * o, part, to(o, 0, d), by_second)

    def share(o, a):
        line = (me.X(a), slice(None)) if o == 0 else (slice(None), me.Y(a))
        ref = W.at[line + (me.c, pl.ds(part * o, part))]
        net.send(ref, ref, me.sib(), by_shared, shared)

    for d in (1, -1, 2):
        for o in (0, 1):
            first[o, d] = push(own, part * o, part, to(o, d, 0), by_first)
    for o in (0, 1):
        over(o, 0)
    yield
    for d in (1, -1, 2):
        for o in (0, 1):
            first[o, d].wait_recv()
            over(o, -d)
    yield
    for k, a in enumerate((0, -1, 1, -2)):
        for o, d in both:
            second[o, a, d].wait_recv()
            start = part * o + (0 if d == 1 else quarter)
            push(block(o, a, -d), start, quarter, to(o, 0, d), by_far, far[k])
        yield
    for k, a in enumerate((0, -1, 1, -2)):
        net.wait(far[k], block_ref)
        for o in (0, 1):
            share(o, a)
    yield
    net.wait(shared, W.at[:, :, 1 - me.c])


def scatter_plane(net, me, S, M1, F1, Q, F2, result):
    half_rows = S.shape[2] // 2

    def index(o, d):
        return me.X(d) if o == 0 else me.Y(d)

    def other(o, d):
        return me.Y(d) if o == 0 else me.X(d)

    def part(o, d, start, size=2):
        rows = pl.ds(half_rows * o, half_rows)
        if o == 0:
            return (index(o, d), pl.ds(start, size), rows)
        return (pl.ds(start, size), index(o, d), rows)

    def to(o, a, b):
        return me.at(*turn(o, a, b))

    both = [(o, d) for d in (1, -1) for o in (0, 1)]
    slot = {1: 0, -1: 1, 2: 2}
    mid = {}
    many, few = net.sender(S.at[pl.ds(0, 3)]), net.sender(F2)
    parts = [net.group() for _ in (0, 1)]
    ends = [net.group() for _ in (0, 1)]
    for o, d in both:
        h = 0 if d == 1 else 2
        mid[o, d] = net.send(S.at[part(o, 2, h)], M1.at[o, slot[d]], to(o, d, 0), many)
    for o, d in both:
        h = 0 if d == 1 else 2
        there = F1.at[o, slot[d], pl.ds(2 - h, 2)]
        net.send(S.at[part(o, d, 2 - h)], there, to(o, d, 0), many, parts[o])
    yield
    for o, d in both:
        h = 0 if d == 1 else 2
        mid[o, d].wait_recv()
        S[part(o, d, h)] += M1[o, slot[d]]
        there = F1.at[o, slot[d], pl.ds(h, 2)]
        net.send(S.at[part(o, d, h)], there, to(o, d, 0), many, parts[o])
    yield
    for o in (0, 1):
        net.wait(parts[o], F1.at[o])
        total = S[part(o, 0, 0, 4)].astype(F32) + F1[o, 0].astype(F32) + F1[o, 1].astype(F32)
        Q[o] = total.astype(BF)
        for d in (1, -1, 2):
            net.send(Q.at[o, other(o, d)], F2.at[o, slot[d]], to(o, 0, d), few, ends[o])
    yield
    for o in (0, 1):
        net.wait(ends[o], F2.at[o])
        result.append(
            (Q[o, other(o, 0)].astype(F32) + F2[o, 0].astype(F32))
            + (F2[o, 1].astype(F32) + F2[o, 2].astype(F32))
        )


def scatter_plane_scratch(rows):
    return [
        pltpu.VMEM((4, 4, 2, rows, COLS), BF),
        pltpu.VMEM((4, 4, rows, COLS), BF),
        pltpu.VMEM((2, 2, 2, rows // 2, COLS), BF),
        pltpu.VMEM((2, 2, 4, rows // 2, COLS), BF),
        pltpu.VMEM((2, 4, rows // 2, COLS), BF),
        pltpu.VMEM((2, 3, rows // 2, COLS), BF),
    ]


class ScatterZ:
    def __init__(self, net, me, T, R):
        self.net, self.me, self.T, self.R = net, me, T, R
        self.sender = net.sender(T.at[pl.ds(0, NZ - 1)])
        self.copies = {}

    def send(self, d, s, piece):
        slot = 0 if d == 1 else 1
        index = self.me.Z(d * (4 - s))
        rows = pl.ds(48 * piece, 48)
        previous = self.copies.get((d, s - 1, piece))
        if previous is not None:
            previous.wait_recv()
            self.T[index, rows] += self.R[slot, s - 1, rows]
        self.copies[d, s, piece] = self.net.send(
            self.T.at[index, rows], self.R.at[slot, s, rows], self.me.up(d), self.sender
        )

    def long(self, s):
        for i in (0, 1):
            self.send(1, s, i)
            self.send(-1, s, 2 + i)

    def short(self, s):
        for i in (0, 1):
            self.send(1, s, 2 + i)
            self.send(-1, s, i)

    def finish(self, V, write):
        for piece in (2, 0, 3, 1):
            rows = pl.ds(48 * piece, 48)
            for d in (1, -1):
                self.copies[d, 3, piece].wait_recv()
            write(
                48 * piece,
                V[rows] + (self.R[0, 3, rows].astype(F32) + self.R[1, 3, rows].astype(F32)),
            )


def exchange(net, me, B1, B2, merge1, merge2):
    row, column = B1.at[pl.ds(1, 7)], B2.at[pl.ds(1, 3)]
    one, two = net.group(), net.group()
    by = net.sender(row), net.sender(column)
    for dy in range(4):
        for dc in range(2):
            if dy + dc > 0:
                net.send(B1.at[0], B1.at[2 * dy + dc], me.at(0, dy, dc), by[0], one)

    def middle():
        net.wait(one, row)
        B2[0] = merge1(B1)
        for dx in range(1, 4):
            net.send(B2.at[0], B2.at[dx], me.at(dx, 0, 0), by[1], two)

    def last():
        net.wait(two, column)
        return merge2(B2)

    return middle, last


def merge_moments(rows):
    def merge(B):
        count = B.shape[0]
        result = []
        for view in range(2):
            means = [B[k, 2 * view : 2 * view + 1] for k in range(count)]
            squares = [B[k, 2 * view + 1 : 2 * view + 2] for k in range(count)]
            mean = sum(means) / count
            square = sum(squares) + rows * sum((m - mean) * (m - mean) for m in means)
            result += [mean, square]
        return jnp.concatenate(result, axis=0)

    return merge


def merge_sums(B):
    return sum(B[k] for k in range(B.shape[0]))


class Pairs:
    def __init__(self, net, me, Pb, S):
        self.net, self.me, self.Pb, self.S = net, me, Pb, S
        self.group, self.sender = net.group(), net.sender(S)
        self.places = []

    def put(self, slot, value):
        rows = pl.ds(16 * slot, 16)
        self.Pb[:, :, :, rows] = value.astype(BF).reshape(4, 4, 2, 16, COLS)
        there = self.S.at[:, :, rows]
        other = self.Pb.at[:, :, 1 - self.me.c, rows]
        self.net.send(other, there, self.me.sib(), self.sender, self.group)
        self.places.append(slot)

    def add(self):
        self.net.wait(self.group, self.S)
        for slot in self.places:
            rows = pl.ds(16 * slot, 16)
            self.S[:, :, rows] += self.Pb[:, :, self.me.c, rows]


class Blocks:
    def __init__(self, net, me, Pb, S):
        self.net, self.me, self.Pb, self.S = net, me, Pb, S
        self.group, self.sender = net.group(), net.sender(S)
        self.places = []

    def where(self, b):
        return (b // 2, pl.ds(2 * (b % 2), 2))

    def put(self, b, value):
        where = self.where(b)
        self.Pb[where] = value.astype(BF).reshape(2, 2, 128, COLS)
        other = self.Pb.at[where + (1 - self.me.c,)]
        self.net.send(other, self.S.at[where], self.me.sib(), self.sender, self.group)
        self.places.append(where)

    def add(self):
        self.net.wait(self.group, self.S)
        for where in self.places:
            self.S[where] += self.Pb[where + (self.me.c,)]


class GatherZ:
    def __init__(self, net, me, A):
        self.net, self.me, self.A = net, me, A
        self.sender = net.sender(A.at[pl.ds(0, NZ - 1), pl.ds(0, ROWS)])
        self.copies = {}

    def order(self):
        return [(1, 0), (-1, 2), (1, 1), (-1, 3), (1, 2), (-1, 0), (1, 3), (-1, 1)]

    def send(self, s, d, piece):
        ref = self.A.at[self.me.Z(-d * s), pl.ds(48 * piece, 48)]
        self.copies[s, d, piece] = self.net.send(ref, ref, self.me.up(d), self.sender)

    def start(self):
        for d, piece in self.order():
            self.send(0, d, piece)

    def step(self, s, places=range(8)):
        for place, (d, piece) in enumerate(self.order()):
            if place in places and (s, d, piece) in self.copies:
                self.copies[s, d, piece].wait_recv()
                if s < 2 or (s == 2 and place < 4):
                    self.send(s + 1, d, piece)


def means(value):
    high = value.astype(BF)
    low = (value - high.astype(F32)).astype(BF)
    rest = jnp.zeros((PAD - ROWS - 2, COLS), BF)
    return jnp.concatenate([high, low, rest], axis=0)


def kernel(
    hf, hs, w, out,
    H, W, acc, DN, A1, A2, B1, B2, X1, X2, Y1, Y2, E, E2, GA, GB, G2, U, T1, R1, T2, R2, V1, V2, PF,
    PA, SA, MA, FA, QA, LA, PB, SB, MB, FB, QB, LB, PG, SG, MG, FG, QG, LG,
    lsem, ssem, rsem,
):
    me = Place()
    net = Net(me, ssem, rsem)
    own = me.block(0, 0)
    mine = (me.x, me.y, me.c)
    loads = [
        pltpu.make_async_copy(w, W.at[mine], lsem.at[0]),
        pltpu.make_async_copy(hf, H.at[pl.ds(0, ROWS)], lsem.at[1]),
        pltpu.make_async_copy(hs, H.at[pl.ds(ROWS, ROWS)], lsem.at[2]),
    ]
    for load in loads:
        load.start()
    barrier(me.plane_peers() + me.z_peers())
    loads[0].wait()
    finish(gather_plane(net, me, W))
    loads[1].wait()
    loads[2].wait()

    acc[...] = jnp.zeros_like(acc)

    def project(k, _):
        cols = pl.ds(pl.multiple_of(k * 1024, 1024), 1024)
        piece = W[k].reshape(1024, COLS)
        acc[...] += jnp.dot(H[:, cols], piece, preferred_element_type=F32)
        return 0

    lax.fori_loop(0, 4, project, 0)

    def view(v):
        return slice(v * ROWS, (v + 1) * ROWS)

    local_mean = []
    for v, B in ((0, B1), (1, B2)):
        mean = jnp.sum(acc[view(v)], axis=0, keepdims=True) / ROWS
        shifted = acc[view(v)] - mean
        X1[0, 2 * v : 2 * v + 1] = mean
        X1[0, 2 * v + 1 : 2 * v + 2] = jnp.sum(shifted * shifted, axis=0, keepdims=True)
        B[me.z] = shifted.astype(BF)
        local_mean.append(mean)
    gz2 = GatherZ(net, me, B2)
    gz1 = GatherZ(net, me, B1)
    middle, last = exchange(net, me, X1, X2, merge_moments(ROWS), merge_moments(8 * ROWS))
    gz2.start()
    middle()
    gz2.step(0)
    moments = last()
    spread, moves = [], []
    for v in range(2):
        spread.append(jnp.sqrt(moments[2 * v + 1 : 2 * v + 2] / TOKENS + epsilon))
        moves.append((local_mean[v] - moments[2 * v : 2 * v + 1], 1.0 / spread[v]))
    E2[0] = jnp.concatenate(moves[1], axis=0)
    scales, scales_by = net.group(), net.sender(E2.at[pl.ds(1, NZ - 1)])
    for d in range(1, NZ):
        net.send(E2.at[0], E2.at[d], me.up(d), scales_by, scales)

    def normalize(A, B, offset, move, scale):
        b = me.Z(offset)
        A[b, 0:ROWS] = ((B[b].astype(F32) + move) * scale).astype(BF)

    def normalize2(slot):
        d = -SLOTS[slot] % NZ
        normalize(A2, B2, SLOTS[slot], E2[d, 0:1], E2[d, 1:2])

    normalize(A1, B1, 0, *moves[0])
    normalize(A2, B2, 0, *moves[1])
    n1, n2 = A1[me.z, 0:ROWS].astype(F32), A2[me.z, 0:ROWS].astype(F32)
    Y1[0, 0:1] = jnp.sum(n1, axis=0, keepdims=True)
    Y1[0, 1:2] = jnp.sum(n2, axis=0, keepdims=True)
    Y1[0, 2:3] = jnp.sum(n1 * n2, axis=0, keepdims=True)
    Y1[0, 3:4] = jnp.zeros((1, COLS), F32)
    middle, last = exchange(net, me, Y1, Y2, merge_sums, merge_sums)
    groups = (Pairs(net, me, PA, SA), Pairs(net, me, PB, SB))

    def correlate(slot):
        if slot > 0:
            normalize2(slot)
        value = dot(A2[me.Z(SLOTS[slot]), 0:ROWS], A1[me.z, 0:ROWS], ((0,), (0,)))
        groups[slot // 4].put(slot % 4, value)

    halves_a, halves_b = [], []
    scatter_a = scatter_plane(net, me, SA, MA, FA, QA, LA, halves_a)
    scatter_b = scatter_plane(net, me, SB, MB, FB, QB, LB, halves_b)
    gz2.step(1, range(4))
    correlate(0)
    gz2.step(1, range(4, 8))
    net.wait(scales, E2.at[pl.ds(1, NZ - 1)])
    correlate(1)
    correlate(2)
    middle()
    gz2.step(2, range(4))
    correlate(3)
    groups[0].add()
    next(scatter_a)
    correlate(4)
    sums = last() / TOKENS
    E[0, 0:2] = sums[0:2]
    E[0, 2:4] = jnp.concatenate(moves[0], axis=0)
    heads = net.group()
    heads_by = net.sender(E.at[pl.ds(1, NZ - 1)])
    for d in range(1, NZ):
        net.send(E.at[0], E.at[d], me.up(d), heads_by, heads)
    gz2.step(2, range(4, 8))
    correlate(5)
    correlate(6)
    next(scatter_a)
    gz2.step(3)
    gz1.start()
    correlate(7)
    groups[1].add()
    next(scatter_b)
    next(scatter_a)
    next(scatter_b)
    diagonal = 2.0 * (sums[2:3] - 1.0)

    def loss_grad(G, halves, group):
        for o in (0, 1):
            rows = pl.ds(32 * o, 32)
            value = (2.0 * offdiag_weight / TOKENS) * halves[o]
            if group == 0 and o == 0:
                row = lax.broadcasted_iota(jnp.int32, (32, COLS), 0)
                column = lax.broadcasted_iota(jnp.int32, (32, COLS), 1)
                same = jnp.logical_and(row < 16, row + 16 * own == column)
                value = jnp.where(same, diagonal, value)
            G[mine + (rows,)] = value.astype(BF)

    turned_ref = G2.at[mine + (pl.ds(0, 112),)]
    turned, turned_by = net.group(), net.sender(turned_ref)

    def turn_over(G, group):
        for k in range(4):
            slot = 4 * group + k
            offset = SLOTS[slot]
            source = G.at[mine + (pl.ds(16 * k, 16),)]
            if offset == 0:
                G2[mine + (pl.ds(0, 16),)] = G[mine + (pl.ds(0, 16),)]
            else:
                there = 7 if offset == 4 else SLOTS.index(-offset)
                target = G2.at[mine + (pl.ds(16 * there, 16),)]
                net.send(source, target, me.up(offset), turned_by, turned)

    finish(scatter_a)
    loss_grad(GA, halves_a, 0)
    gather_a = gather_plane(net, me, GA)
    next(gather_a)
    turn_over(GA, 0)
    gz1.step(0)
    next(scatter_b)
    next(gather_a)
    finish(scatter_b)
    loss_grad(GB, halves_b, 1)
    gather_b = gather_plane(net, me, GB)
    next(gather_b)
    turn_over(GB, 1)
    gz1.step(1)
    advance(gather_a, 4)
    next(gather_b)
    next(gather_a)
    net.wait(heads, E.at[pl.ds(1, NZ - 1)])
    for d in range(NZ):
        A1[me.Z(-d), ROWS:PAD] = means(E[d, 0:1])
        A2[me.Z(-d), ROWS:PAD] = means(E[d, 1:2])
    advance(gather_b, 4)
    net.wait(turned, turned_ref)
    gather_2 = gather_plane(net, me, G2)
    next(gather_2)
    gz1.step(2)
    finish(gather_a)
    ones = jnp.ones((16, COLS), BF)

    def upstream(A, G, slot, dims, start):
        rows = pl.ds(16 * (slot % (G.shape[3] // 16)), 16)
        g = G[:, :, :, rows].reshape(COLS, COLS)
        squares = g * g
        if slot == 0:
            shape = (COLS, COLS)
            same = lax.broadcasted_iota(jnp.int32, shape, 0) == lax.broadcasted_iota(
                jnp.int32, shape, 1
            )
            squares = jnp.where(same, 0.0, squares.astype(F32)).astype(BF)
        u = dot(A[me.Z(SLOTS[slot])], g, ((1,), dims))
        s = dot(ones, squares, ((1,), dims))[0:8]
        if start:
            U[0:PAD] = u
            U[PAD : PAD + 8] = s
        else:
            U[0:PAD] += u
            U[PAD : PAD + 8] += s

    own_slope = diagonal.astype(BF).astype(F32) * sums[2:3]

    def down(v, A):
        level = U[ROWS : ROWS + 1] + U[ROWS + 1 : ROWS + 2]
        slope = U[PAD : PAD + 1] * (0.5 / offdiag_weight) + own_slope
        n = A[me.z, 0:ROWS].astype(F32)
        DN[view(v)] = ((U[0:ROWS] - level - n * slope) / spread[v]).astype(BF)

    def partial(v, T, V, d):
        b = me.Z(d)
        piece = W[lax.div(b, 2), pl.ds(2 * lax.rem(b, 2), 2)].reshape(COLS, COLS)
        t = dot(DN[view(v)], piece, ((1,), (1,)))
        if d == 0:
            V[...] = t
        else:
            T[b] = t.astype(BF)

    for slot in range(4):
        upstream(A2, GA, slot, (0,), slot == 0)
    next(gather_b)
    next(gather_2)
    finish(gather_b)
    for slot in range(4, 8):
        upstream(A2, GB, slot, (0,), False)
    down(0, A1)
    ring1 = ScatterZ(net, me, T1, R1)
    ring2 = ScatterZ(net, me, T2, R2)

    def weight_first(b):
        PF[b] = dot(H[0:ROWS, pl.ds(b * COLS, COLS)], DN[0:ROWS], ((0,), (0,)))

    partial(0, T1, V1, 4)
    ring1.long(0)
    partial(0, T1, V1, 3)
    partial(0, T1, V1, -3)
    ring1.short(1)
    next(gather_2)
    partial(0, T1, V1, 2)
    partial(0, T1, V1, -2)
    gz1.step(3)
    next(gather_2)
    weight_first(0)
    weight_first(1)
    ring1.long(1)
    next(gather_2)
    partial(0, T1, V1, 1)
    partial(0, T1, V1, -1)
    ring1.short(2)
    next(gather_2)
    weight_first(2)
    weight_first(3)
    partial(0, T1, V1, 0)
    ring1.long(2)
    weight_first(4)
    weight_first(5)
    for slot in range(1, 8):
        d = -SLOTS[slot] % NZ
        normalize(A1, B1, SLOTS[slot], E[d, 2:3], E[d, 3:4])
    next(gather_2)
    ring1.short(3)
    weight_first(6)
    weight_first(7)
    ring1.long(3)
    finish(gather_2)
    for slot in range(8):
        upstream(A1, G2, slot, (1,), slot == 0)
    down(1, A2)
    def writer(start):
        def write(row, value):
            out[start + row : start + row + 48] = value.astype(BF)

        return write

    partial(1, T2, V2, 4)
    ring2.long(0)
    weight = Blocks(net, me, PG, SG)
    for b in range(8):
        second = dot(
            H[ROWS : 2 * ROWS, pl.ds(b * COLS, COLS)], DN[ROWS : 2 * ROWS], ((0,), (0,))
        )
        weight.put(b, PF[b] + second)
        if b == 3:
            partial(1, T2, V2, 3)
            partial(1, T2, V2, -3)
            ring2.short(1)
    weight.add()
    halves_g = []
    scatter_g = scatter_plane(net, me, SG, MG, FG, QG, LG, halves_g)
    next(scatter_g)
    partial(1, T2, V2, 2)
    partial(1, T2, V2, -2)
    ring2.long(1)
    partial(1, T2, V2, 1)
    partial(1, T2, V2, -1)
    ring2.short(2)
    next(scatter_g)
    partial(1, T2, V2, 0)
    ring2.long(2)
    ring1.finish(V1, writer(128))
    ring2.short(3)
    next(scatter_g)
    ring2.long(3)
    ring2.finish(V2, writer(128 + ROWS))
    finish(scatter_g)
    for o in (0, 1):
        out[64 * o : 64 * o + 64] = (halves_g[o] / math.sqrt(TOKENS)).astype(BF)
    net.drain()


def local(hidden_first, hidden_second, weight):
    vm = pl.BlockSpec(memory_space=pltpu.VMEM)
    hbm = pl.BlockSpec(memory_space=pl.ANY)
    senders, count = 36, 254
    out = pl.pallas_call(
        kernel,
        out_shape=jax.ShapeDtypeStruct((128 + 2 * ROWS, COLS), BF),
        in_specs=[hbm] * 3,
        out_specs=vm,
        scratch_shapes=[
            pltpu.VMEM((2 * ROWS, 4096), BF),
            pltpu.VMEM((4, 4, 2, 128, COLS), BF),
            pltpu.VMEM((2 * ROWS, COLS), F32),
            pltpu.VMEM((2 * ROWS, COLS), BF),
            pltpu.VMEM((NZ, PAD, COLS), BF),
            pltpu.VMEM((NZ, PAD, COLS), BF),
            pltpu.VMEM((NZ, ROWS, COLS), BF),
            pltpu.VMEM((NZ, ROWS, COLS), BF),
            pltpu.VMEM((8, 4, COLS), F32),
            pltpu.VMEM((4, 4, COLS), F32),
            pltpu.VMEM((8, 4, COLS), F32),
            pltpu.VMEM((4, 4, COLS), F32),
            pltpu.VMEM((NZ, 4, COLS), F32),
            pltpu.VMEM((NZ, 2, COLS), F32),
            pltpu.VMEM((4, 4, 2, 64, COLS), BF),
            pltpu.VMEM((4, 4, 2, 64, COLS), BF),
            pltpu.VMEM((4, 4, 2, 128, COLS), BF),
            pltpu.VMEM((PAD + 8, COLS), F32),
            pltpu.VMEM((NZ, ROWS, COLS), BF),
            pltpu.VMEM((2, 4, ROWS, COLS), BF),
            pltpu.VMEM((NZ, ROWS, COLS), BF),
            pltpu.VMEM((2, 4, ROWS, COLS), BF),
            pltpu.VMEM((ROWS, COLS), F32),
            pltpu.VMEM((ROWS, COLS), F32),
            pltpu.VMEM((8, COLS, COLS), F32),
        ]
        + scatter_plane_scratch(64)
        + scatter_plane_scratch(64)
        + scatter_plane_scratch(128)
        + [
            pltpu.SemaphoreType.DMA((3,)),
            pltpu.SemaphoreType.DMA((senders,)),
            pltpu.SemaphoreType.DMA((count,)),
        ],
        compiler_params=pltpu.CompilerParams(
            collective_id=1, has_side_effects=True, vmem_limit_bytes=60 * 1024 * 1024
        ),
    )(hidden_first, hidden_second, weight)
    return out[:128], out[128 : 128 + ROWS], out[128 + ROWS :]


def solution(mesh):
    in_specs = (P("dp", None), P("dp", None), P("dp", "mp"))
    out_specs = (P("dp", "mp"), P("dp", "mp"), P("dp", "mp"))
    return jax.shard_map(local, mesh=mesh, in_specs=in_specs, out_specs=out_specs, check_vma=False)
```
